32 devices in a mesh: section: 2 (over core), row: 4 (over z), col: 4 (over y, x).
Axes of the slice: x: 2, y: 2, z: 4, core: 2. Of those that a mesh axis runs over, the one named last changes fastest.
Arguments:
- inputs: bfloat16 [2, 2048, 1536], P(None, 'row'), may hold values from -6 to 6
- positions: int32 [2, 2048], P(None, 'row'), may hold values from 0 to 7165, as said below
- w_query: bfloat16 [2, 1536, 1536], P('section', 'row', 'col'), may hold values from -0.15625 to 0.15625
- key_weight: bfloat16 [2, 1536, 768], P('section', 'row', 'col'), may hold values from -0.15625 to 0.15625
- value_weight: bfloat16 [2, 1536, 768], P('section', 'row', 'col'), may hold values from -0.15625 to 0.15625
- w_out: bfloat16 [2, 1536, 1536], P('section', 'row', 'col'), may hold values from -2.5 to 2.5
- w_gate: bfloat16 [2, 1536, 4096], P('section', 'row', 'col'), may hold values from -0.15625 to 0.15625
- w_up: bfloat16 [2, 1536, 4096], P('section', 'row', 'col'), may hold values from -0.15625 to 0.15625
- w_down: bfloat16 [2, 1536, 4096], P('section', 'row', 'col'), may hold values from -0.1875 to 0.1875
- gain_attn: bfloat16 [2, 1536], P('section', 'row'), may hold values from 0.25 to 1.75
- gain_ffn: bfloat16 [2, 1536], P('section', 'row'), may hold values from 0.25 to 1.75
- cotangent: bfloat16 [2, 2048, 1536], P(None, 'row'), may hold values from -6 to 6
Outputs:
- activations: bfloat16 [2, 2, 2048, 1536], P('section', None, 'row')
- input_grads: bfloat16 [2, 2, 2048, 1536], P('section', None, 'row')
- grad_w_query: float32 [2, 1536, 1536], P('section', 'row', 'col')
- grad_w_key: float32 [2, 1536, 768], P('section', 'row', 'col')
- grad_w_value: float32 [2, 1536, 768], P('section', 'row', 'col')
- grad_w_out: float32 [2, 1536, 1536], P('section', 'row', 'col')
- grad_w_gate: float32 [2, 1536, 4096], P('section', 'row', 'col')
- grad_w_up: float32 [2, 1536, 4096], P('section', 'row', 'col')
- grad_w_down: float32 [2, 1536, 4096], P('section', 'row', 'col')
- grad_gain_attn: float32 [2, 1536], P('section', 'row')
- grad_gain_ffn: float32 [2, 1536], P('section', 'row')
The draws below stay inside these ranges and needn't reach their ends.
Inputs may be any that keep to these rules, and one draw needn't show every extreme that they name: A sequence's rows form four blocks of 256; in the sequence's order they stand first, third, fourth, second, and along that order the positions rise by 1 to 3 from token to token. The first sequence of micro-batch 0 starts at 0; the last one of the last micro-batch ends at 7165.
All inputs are finite; a program needn't handle non-finite values.
Results may differ from the reference program's by a relative error of at most 0.03.
Values may be sent and summed in bfloat16 or wider, within the bound.
No kernel may reach another device: no remote copies, remote signals or barrier semaphores. Data moves between devices by JAX's collectives and lax.ppermute only.
A program may use at most 192 MiB of HBM per device.

```python
import math
import jax
import jax.numpy as jnp
from jax import lax

D = 1536
QUERY_HEADS = 16
KEY_VALUE_HEADS = 8
HEAD_SIZE = 96
FF = 4096
MICRO = 2
QUERY_FEATURES = 1536
KW = 768
SEQUENCE_LENGTH = 1024
SEQS = 2
TOKENS = 2048
N_SECTION = 2


def draw_positions(key, part):
    start_key, step_key = jax.random.split(key)
    steps = jax.random.randint(step_key, (MICRO, SEQS, SEQUENCE_LENGTH), 1, 4).astype(jnp.int32)
    steps = steps.at[:, :, 0].set(0)
    climbs = jnp.cumsum(steps, axis=-1).astype(jnp.int32)
    starts = jax.random.randint(start_key, (MICRO, SEQS), 0, 4 * SEQUENCE_LENGTH + 1).astype(jnp.int32)
    last_start = 7 * SEQUENCE_LENGTH - 3 - climbs[MICRO - 1, SEQS - 1, SEQUENCE_LENGTH - 1]
    starts = starts.at[0, 0].set(0).at[MICRO - 1, SEQS - 1].set(last_start)
    ordered = starts[:, :, None] + climbs
    quarter = SEQUENCE_LENGTH // 4
    arranged = jnp.concatenate([ordered[:, :, 0:quarter], ordered[:, :, 3 * quarter:4 * quarter], ordered[:, :, quarter:2 * quarter], ordered[:, :, 2 * quarter:3 * quarter]], axis=-1)
    return arranged.reshape(MICRO, SEQS * SEQUENCE_LENGTH).astype(jnp.int32)


def block_scale(key, extent, cuts, least, high):
    loudness, own = 1.0, jax.random.fold_in(key, 6)
    for position, blocks in cuts:
        draws = jnp.exp(jax.random.uniform(jax.random.fold_in(own, position), (blocks,), jnp.float32, least / len(cuts), high / len(cuts)))
        loudness = loudness * jnp.repeat(draws, extent[position] // blocks).reshape([-1 if axis == position else 1 for axis in range(len(extent))])
    return loudness


def centred(stream_key, shape, deviation, limit, shards=(), kind=jnp.bfloat16):
    gain = block_scale(stream_key, shape, shards, -0.22, 0.18) if shards else 1.0
    values = jax.random.normal(stream_key, shape, jnp.float32) * deviation * gain
    return jnp.minimum(jnp.maximum(values, -limit), limit).astype(kind)


def setup_inputs(seed: int = 0) -> dict:
    seeds = jax.random.split(jax.random.key(seed), 13)
    inputs = centred(seeds[0], (MICRO, TOKENS, D), 1.0, 6.0, ((1, 4),))
    positions = draw_positions(jax.random.fold_in(seeds[12], 71), 0)
    w_query = centred(seeds[2], (N_SECTION, D, QUERY_FEATURES), D ** -0.5, 0.15625, ((0, 2), (1, 4), (2, 4)))
    key_weight = centred(seeds[3], (N_SECTION, D, KW), D ** -0.5, 0.15625, ((0, 2), (1, 4), (2, 4)))
    value_weight = centred(seeds[4], (N_SECTION, D, KW), D ** -0.5, 0.15625, ((0, 2), (1, 4), (2, 4)))
    w_out = centred(seeds[5], (N_SECTION, D, QUERY_FEATURES), (QUERY_FEATURES * 4 // SEQUENCE_LENGTH) ** -0.5, 2.5, ((0, 2), (1, 4), (2, 4)))
    w_gate = centred(seeds[6], (N_SECTION, D, FF), D ** -0.5, 0.15625, ((0, 2), (1, 4), (2, 4)))
    w_up = centred(seeds[7], (N_SECTION, D, FF), D ** -0.5, 0.15625, ((0, 2), (1, 4), (2, 4)))
    w_down = centred(seeds[8], (N_SECTION, D, FF), (FF // 4) ** -0.5, 0.1875, ((0, 2), (1, 4), (2, 4)))
    gain_attn = jnp.clip(1.0 + 0.15 * jax.random.normal(seeds[9], (N_SECTION, D), jnp.float32), 0.25, 1.75).astype(jnp.bfloat16)
    gain_ffn = jnp.clip(1.0 + 0.15 * jax.random.normal(seeds[10], (N_SECTION, D), jnp.float32), 0.25, 1.75).astype(jnp.bfloat16)
    cotangent = centred(seeds[11], (MICRO, TOKENS, D), 1.0, 6.0, ((1, 4),))
    return {"inputs": inputs, "positions": positions, "w_query": w_query, "key_weight": key_weight, "value_weight": value_weight, "w_out": w_out, "w_gate": w_gate, "w_up": w_up, "w_down": w_down, "gain_attn": gain_attn, "gain_ffn": gain_ffn, "cotangent": cotangent}


@jax.custom_vjp
def low(v):
    return lax.optimization_barrier(v.astype(jnp.bfloat16)).astype(jnp.float32)

@jax.custom_vjp
def low_back(v):
    return v

def low_keep(v):
    return (low(v), None)

def low_pass(kept, grad):
    return (grad,)

def back_keep(v):
    return (v, None)

def back_low(kept, grad):
    return (low(grad),)
low.defvjp(low_keep, low_pass)
low_back.defvjp(back_keep, back_low)
EPSILON = 1e-05
ROPE_BASE = 100000.0
MASKED = -1e+30

def matrix_product(left, right):
    return jnp.dot(left, right, precision=lax.Precision.HIGHEST)

def rotation(position_ids):
    half_dim = HEAD_SIZE // 2
    inverse = ROPE_BASE ** (-(jnp.arange(half_dim, dtype=jnp.float32) * 2.0) / HEAD_SIZE)
    angles = position_ids.astype(jnp.float32)[:, None] * inverse[None, :]
    return (jnp.cos(angles), jnp.sin(angles))

def rotate(values, cosine_table, sine_table):
    half_dim = values.shape[-1] // 2
    first_half = values[..., :half_dim]
    second_half = values[..., half_dim:]
    cos_here = cosine_table[:, None, :]
    sin_here = sine_table[:, None, :]
    return jnp.concatenate([first_half * cos_here - second_half * sin_here, second_half * cos_here + first_half * sin_here], axis=-1)

def sequence_attend(sequence_item):
    query_rows, keys_all, values, place_seq = sequence_item
    group_rows = query_rows.reshape(SEQUENCE_LENGTH, KEY_VALUE_HEADS, QUERY_HEADS // KEY_VALUE_HEADS, HEAD_SIZE)
    scores = jnp.einsum('qgrd,kgd->grqk', group_rows, keys_all, precision=lax.Precision.HIGHEST) * (1.0 / math.sqrt(HEAD_SIZE))
    scores = low_back(scores)
    causal = place_seq[None, :] <= place_seq[:, None]
    scores = jnp.where(causal, scores, MASKED)
    row_peak = lax.optimization_barrier(jnp.max(scores, axis=-1, keepdims=True))
    weights = jnp.exp(scores - row_peak)
    probs_low = low(weights / lax.optimization_barrier(jnp.sum(weights, axis=-1, keepdims=True)))
    merged_heads = jnp.einsum('grqk,kgd->qgrd', probs_low, values, precision=lax.Precision.HIGHEST)
    return merged_heads.reshape(SEQUENCE_LENGTH, QUERY_HEADS * HEAD_SIZE)

def layer(hidden_in, cosine_table, sine_table, place_all, params):
    w_query, key_weight, value_weight, w_out, w_gate, w_up, w_down, gain_attn, gain_ffn = params
    count_tokens = hidden_in.shape[0]
    sequence_count = count_tokens // SEQUENCE_LENGTH
    scale_one = lax.rsqrt(lax.optimization_barrier(jnp.mean(hidden_in * hidden_in, axis=-1, keepdims=True)) + EPSILON)
    norm_rows = low(hidden_in * scale_one * gain_attn)
    query_raw = low_back(matrix_product(norm_rows, w_query)).reshape(count_tokens, QUERY_HEADS, HEAD_SIZE)
    key_unrotated = low_back(matrix_product(norm_rows, key_weight)).reshape(count_tokens, KEY_VALUE_HEADS, HEAD_SIZE)
    value_projected = low(low_back(matrix_product(norm_rows, value_weight))).reshape(count_tokens, KEY_VALUE_HEADS, HEAD_SIZE)
    query_rotated = low(rotate(query_raw, cosine_table, sine_table))
    key_rotated = low(rotate(key_unrotated, cosine_table, sine_table))
    merged_heads = lax.map(jax.checkpoint(sequence_attend), (query_rotated.reshape(sequence_count, SEQUENCE_LENGTH, QUERY_HEADS, HEAD_SIZE), key_rotated.reshape(sequence_count, SEQUENCE_LENGTH, KEY_VALUE_HEADS, HEAD_SIZE), value_projected.reshape(sequence_count, SEQUENCE_LENGTH, KEY_VALUE_HEADS, HEAD_SIZE), place_all.reshape(sequence_count, SEQUENCE_LENGTH)))
    merged_heads = low(low_back(merged_heads.reshape(count_tokens, QUERY_HEADS * HEAD_SIZE)))
    middle = hidden_in + low_back(matrix_product(merged_heads, w_out.T))
    scale_two = lax.rsqrt(lax.optimization_barrier(jnp.mean(middle * middle, axis=-1, keepdims=True)) + EPSILON)
    normed_two = low(middle * scale_two * gain_ffn)
    gate_proj = low_back(matrix_product(normed_two, w_gate))
    up_proj = low_back(matrix_product(normed_two, w_up))
    hidden = low(jax.nn.silu(gate_proj) * up_proj)
    return middle + low_back(matrix_product(hidden, w_down.T))

def forward(start_in, probes, cosine_table, sine_table, place_all, params_all):
    hidden_in = start_in
    outputs = []
    for section_index in range(N_SECTION):
        hidden_in = hidden_in + probes[section_index]
        result = layer(hidden_in, cosine_table, sine_table, place_all, [tensor[section_index] for tensor in params_all])
        hidden_in = low(low_back(result))
        outputs.append(hidden_in)
    return jnp.stack(outputs)

def reference(inputs, positions, w_query, key_weight, value_weight, w_out, w_gate, w_up, w_down, gain_attn, gain_ffn, cotangent):
    count_tokens = MICRO * TOKENS
    start_in = inputs.astype(jnp.float32).reshape(count_tokens, D)
    place_all = positions.reshape(count_tokens).astype(jnp.int32)
    cosine_table, sine_table = rotation(place_all)
    params_all = tuple((tensor.astype(jnp.float32) for tensor in (w_query, key_weight, value_weight, w_out, w_gate, w_up, w_down, gain_attn, gain_ffn)))
    probes = jnp.zeros((N_SECTION, count_tokens, D), jnp.float32)

    def wrapped(start_value, probe_values, params_value):
        return forward(start_value, probe_values, cosine_table, sine_table, place_all, params_value)
    outputs, pullback = jax.vjp(wrapped, start_in, probes, params_all)
    seed_grads = jnp.zeros((N_SECTION, count_tokens, D), jnp.float32).at[N_SECTION - 1].set(cotangent.astype(jnp.float32).reshape(count_tokens, D))
    grad_start, grad_probes, grad_params = pullback(seed_grads)
    g_query, g_key, g_value, g_out, g_gate, g_up, g_down, g_gain_attn, g_gain_ffn = grad_params
    activations = outputs.reshape(N_SECTION, MICRO, TOKENS, D).astype(jnp.bfloat16)
    input_grads = grad_probes.reshape(N_SECTION, MICRO, TOKENS, D).astype(jnp.bfloat16)
    return (activations, input_grads, g_query, g_key, g_value, g_out, g_gate, g_up, g_down, g_gain_attn, g_gain_ffn)
```

```python
import math

import jax
import jax.numpy as jnp
from jax import lax
from jax.sharding import PartitionSpec as P

HEAD_SIZE = 96
HALF = HEAD_SIZE // 2
EPSILON = 1e-05
ROPE_BASE = 100000.0
MASKED = -1e30
BF = jnp.bfloat16
F32 = jnp.float32


def mate(x, axis, k):
    n = lax.axis_size(axis)
    return lax.ppermute(x, axis, [(j, j ^ k) for j in range(n)])


def ring(x, by):
    n = lax.axis_size("row")
    return lax.ppermute(x, "row", [(j, (j + by) % n) for j in range(n)])


def rotation(position_ids):
    inverse = ROPE_BASE ** (-(jnp.arange(HALF, dtype=F32) * 2.0) / HEAD_SIZE)
    angles = position_ids.astype(F32)[:, None] * inverse[None, :]
    return (jnp.cos(angles), jnp.sin(angles))


def rotate(values, tables, sign):
    cos_here, sin_here = tables[0][:, None, :], tables[1][:, None, :] * sign
    first, second = values[..., :HALF], values[..., HALF:]
    return jnp.concatenate(
        [first * cos_here - second * sin_here, second * cos_here + first * sin_here], axis=-1
    )


def dot(left, right):
    return jnp.dot(left, right, preferred_element_type=F32)


def dot_t(left, right):
    return lax.dot_general(left, right, (((1,), (1,)), ((), ())), preferred_element_type=F32)


def t_dot(left, right):
    return lax.dot_general(left, right, (((0,), (0,)), ((), ())), preferred_element_type=F32)


def roll_features(x, blocks):
    width = x.shape[-1]
    n = lax.axis_size("row")
    return lax.dynamic_slice_in_dim(
        jnp.concatenate([x, x], -1), (blocks % n) * (width // n), width, x.ndim - 1
    )


def sum_scatter(partial):
    n = lax.axis_size("col")
    c = lax.axis_index("col")
    rows = partial.shape[0] // n

    def piece(k):
        return lax.dynamic_slice_in_dim(partial, (c ^ k) * rows, rows, 0)

    total = piece(0).astype(F32)
    for k in range(1, n):
        total = total + mate(piece(k), "col", k).astype(F32)
    return total


def gather_rows(local):
    n = lax.axis_size("col")
    c = lax.axis_index("col")
    slots = [local] + [mate(local, "col", k) for k in range(1, n)]
    out = jnp.zeros((n * local.shape[0], local.shape[1]), local.dtype)
    for k in range(n):
        out = lax.dynamic_update_slice_in_dim(out, slots[k], (c ^ k) * local.shape[0], 0)
    return out


def own_rows(x):
    rows = x.shape[0] // lax.axis_size("col")
    return lax.dynamic_slice_in_dim(x, lax.axis_index("col") * rows, rows, 0)


def allowed(rows):
    half = rows // 2
    parity = lax.axis_index("row") % 2
    offsets = jnp.arange(rows)

    def order_of(side):
        return offsets + jnp.where(side == 0, jnp.where(offsets < half, 0, 2 * half), half)

    own, other = order_of(parity), order_of(1 - parity)
    return jnp.concatenate([other, own])[None, :] <= own[:, None]


def attend(query, keys, values, mask):
    scores = jnp.einsum("qgrd,kgd->grqk", query, keys, preferred_element_type=F32)
    scores = jnp.where(mask, scores * (1.0 / math.sqrt(HEAD_SIZE)), MASKED)
    peak = jnp.max(scores, axis=-1, keepdims=True)
    weights = jnp.exp(scores - peak)
    total = jnp.sum(weights, axis=-1, keepdims=True)
    probs = (weights / total).astype(BF)
    mixed = jnp.einsum("grqk,kgd->qgrd", probs, values, preferred_element_type=F32)
    return mixed.astype(BF), peak + jnp.log(total)


def attend_back(query, keys, values, log_sums, grad_mixed, mask):
    scale = 1.0 / math.sqrt(HEAD_SIZE)
    scores = jnp.einsum("qgrd,kgd->grqk", query, keys, preferred_element_type=F32)
    scores = jnp.where(mask, scores * scale, MASKED)
    probs = jnp.exp(scores - log_sums)
    grad_probs = jnp.einsum("qgrd,kgd->grqk", grad_mixed, values, preferred_element_type=F32)
    inner = jnp.sum(probs * grad_probs, axis=-1, keepdims=True)
    grad_scores = (probs * (grad_probs - inner)).astype(BF)
    grad_query = jnp.einsum("grqk,kgd->qgrd", grad_scores, keys, preferred_element_type=F32)
    grad_keys = jnp.einsum("grqk,qgrd->kgd", grad_scores, query, preferred_element_type=F32)
    grad_values = jnp.einsum(
        "grqk,qgrd->kgd", probs.astype(BF), grad_mixed, preferred_element_type=F32
    )
    return grad_query * scale, grad_keys * scale, grad_values


def halves(w):
    width = w.shape[1] // 2
    return [w[:, :width], w[:, width:]]


def gather_weights(own_attn, own_ffn):
    s = lax.axis_index("section")
    n = lax.axis_size("row")
    layers = []
    for parts in (own_attn, own_ffn):
        keep = jnp.where(s == 0, parts[0], parts[1])
        got = mate(jnp.where(s == 0, parts[1], parts[0]), "section", 1)
        layers.append([jnp.where(s == layer, keep, got) for layer in range(2)])
    out = []
    for layer in range(2):
        groups = []
        for group in range(2):
            slots = [layers[group][layer]]
            for _ in range(1, n):
                slots.append(ring(slots[-1], -1))
            others = [mate(x, "section", 1) for x in slots]
            groups.append((jnp.concatenate(slots, 0), jnp.concatenate(others, 0)))
        out.append(groups)
    return out


def layer_weights(groups, kv, qw, ff):
    (am, ao), (fm, fo) = groups

    def both(m, o, start, width):
        return jnp.concatenate([m[:, start : start + width], o[:, start : start + width]], 1)

    return dict(
        w_query=both(am, ao, 0, qw),
        w_key=both(am, ao, qw, kv),
        w_value=both(am, ao, qw + kv, kv),
        w_out=both(am, ao, qw + 2 * kv, qw),
        gain_attn=am[:, -2].astype(F32)[None, :],
        gain_ffn=am[:, -1].astype(F32)[None, :],
        w_gate=both(fm, fo, 0, ff),
        w_up=both(fm, fo, ff, ff),
        w_down=both(fm, fo, 2 * ff, ff),
    )


def layer_forward(x, tables, w, mask):
    rows = x.shape[0]
    groups = w["w_query"].shape[1] // w["w_key"].shape[1]
    kv_heads = w["w_key"].shape[1] // HEAD_SIZE
    xf = x.astype(F32)
    r1 = lax.rsqrt(jnp.mean(xf * xf, axis=-1, keepdims=True) + EPSILON)
    n1 = (xf * r1 * w["gain_attn"]).astype(BF)
    query = dot(n1, w["w_query"]).reshape(rows, -1, HEAD_SIZE)
    key = dot(n1, w["w_key"]).reshape(rows, -1, HEAD_SIZE)
    value = dot(n1, w["w_value"]).astype(BF).reshape(rows, -1, HEAD_SIZE)
    query = rotate(query, tables, 1.0).astype(BF).reshape(rows, kv_heads, groups, HEAD_SIZE)
    key = rotate(key, tables, 1.0).astype(BF)
    both = jnp.concatenate([key, value], 1)
    there = mate(both, "row", 1)
    keys = jnp.concatenate([there[:, :kv_heads], key], 0)
    values = jnp.concatenate([there[:, kv_heads:], value], 0)
    mixed, log_sums = attend(query, keys, values, mask)
    mixed = mixed.reshape(rows, -1)
    middle = own_rows(xf) + sum_scatter(dot_t(mixed, w["w_out"]).astype(BF))
    r2 = lax.rsqrt(jnp.mean(middle * middle, axis=-1, keepdims=True) + EPSILON)
    n2 = gather_rows((middle * r2 * w["gain_ffn"]).astype(BF))
    gate = dot(n2, w["w_gate"])
    up = dot(n2, w["w_up"])
    hidden = (jax.nn.silu(gate) * up).astype(BF)
    y = (middle + sum_scatter(dot_t(hidden, w["w_down"]).astype(BF))).astype(BF)
    out = gather_rows(y)
    kept = (own_rows(xf), own_rows(r1), n1, query, keys, values, mixed, log_sums)
    return out, kept + (middle, r2, n2, gate, up, hidden)


def layer_backward(kept, grad_out, tables, w, mask):
    (x, r1, n1, query, keys, values, mixed, log_sums, middle, r2, n2, gate, up, hidden) = kept
    rows = grad_out.shape[0]
    grad_hidden = dot(grad_out, w["w_down"])
    g_down = t_dot(grad_out, hidden)
    sig = jax.nn.sigmoid(gate)
    grad_gate = (grad_hidden * up * sig * (1.0 + gate * (1.0 - sig))).astype(BF)
    grad_up = (grad_hidden * gate * sig).astype(BF)
    g_gate = t_dot(n2, grad_gate)
    g_up = t_dot(n2, grad_up)
    grad_n2 = sum_scatter(
        (dot_t(grad_gate, w["w_gate"]) + dot_t(grad_up, w["w_up"])).astype(BF)
    )
    unit = middle * r2
    scaled = grad_n2 * w["gain_ffn"]
    g_gain_ffn = jnp.sum(grad_n2 * unit, axis=0)
    grad_middle = own_rows(grad_out).astype(F32) + r2 * (
        scaled - unit * jnp.mean(scaled * unit, axis=-1, keepdims=True)
    )
    grad_attn = gather_rows(grad_middle.astype(BF))
    grad_mixed = dot(grad_attn, w["w_out"]).astype(BF).reshape(query.shape)
    g_out = t_dot(grad_attn, mixed)
    grad_query, grad_keys, grad_values = attend_back(
        query, keys, values, log_sums, grad_mixed, mask
    )
    back = mate(
        jnp.concatenate([grad_keys[:rows], grad_values[:rows]], 1).astype(BF), "row", 1
    ).astype(F32)
    kv_heads = keys.shape[1]
    grad_key = grad_keys[rows:] + back[:, :kv_heads]
    grad_value = (grad_values[rows:] + back[:, kv_heads:]).astype(BF).reshape(rows, -1)
    grad_query = rotate(grad_query.reshape(rows, -1, HEAD_SIZE), tables, -1.0)
    grad_query = grad_query.astype(BF).reshape(rows, -1)
    grad_key = rotate(grad_key, tables, -1.0).astype(BF).reshape(rows, -1)
    g_query = t_dot(n1, grad_query)
    g_key = t_dot(n1, grad_key)
    g_value = t_dot(n1, grad_value)
    grad_n1 = sum_scatter(
        (
            dot_t(grad_query, w["w_query"])
            + dot_t(grad_key, w["w_key"])
            + dot_t(grad_value, w["w_value"])
        ).astype(BF)
    )
    unit = x * r1
    scaled = grad_n1 * w["gain_attn"]
    g_gain_attn = jnp.sum(grad_n1 * unit, axis=0)
    grad_x = grad_middle + r1 * (
        scaled - unit * jnp.mean(scaled * unit, axis=-1, keepdims=True)
    )
    grad_x = gather_rows(grad_x.astype(BF))

    def split(parts):
        return [
            jnp.concatenate([halves(p)[h] for p in parts], 1).astype(BF) for h in range(2)
        ]

    attn = split([g_query, g_key, g_value, g_out])
    ffn = split([g_gate, g_up, g_down])
    return grad_x, attn, ffn, (g_gain_attn, g_gain_ffn)


def reduce_grads(mine, other):
    n = lax.axis_size("row")
    got = mate(other, "section", 1)
    total = mine.astype(F32) + got.astype(F32)
    rows = total.shape[0] // n

    def slot(k):
        return total[k * rows : (k + 1) * rows]

    moving = slot(n - 1).astype(BF)
    for t in range(1, n):
        got = ring(moving, 1).astype(F32)
        here = slot(n - 1 - t) + got
        moving = here.astype(BF)
    return here


def reduce_gains(gains):
    s = lax.axis_index("section")
    n = lax.axis_size("row")
    total = gains
    for k in range(1, lax.axis_size("col")):
        total = total + mate(gains, "col", k)
    width = gains.shape[1] // n
    here = total[:, :width]
    for k in range(1, n):
        here = here + ring(total[:, k * width : (k + 1) * width], k)
    keep = jnp.where(s == 0, here[:2], here[2:])
    send = jnp.where(s == 0, here[2:], here[:2])
    return keep + mate(send, "section", 1)


def body(
    inputs,
    positions,
    w_query,
    key_weight,
    value_weight,
    w_out,
    w_gate,
    w_up,
    w_down,
    gain_attn,
    gain_ffn,
    cotangent,
):
    s = lax.axis_index("section")
    row = lax.axis_index("row")
    half_q, half_kv, half_ff = (
        w_query.shape[2] // 2,
        key_weight.shape[2] // 2,
        w_gate.shape[2] // 2,
    )
    gains = [gain_attn[0][:, None], gain_ffn[0][:, None]]
    own_attn = [
        jnp.concatenate(
            [halves(p[0])[h] for p in (w_query, key_weight, value_weight, w_out)] + gains, 1
        )
        for h in range(2)
    ]
    own_ffn = [
        jnp.concatenate([halves(p[0])[h] for p in (w_gate, w_up, w_down)], 1) for h in range(2)
    ]
    gathered = gather_weights(own_attn, own_ffn)
    weights = [layer_weights(g, half_kv, half_q, half_ff) for g in gathered]
    x = lax.dynamic_index_in_dim(inputs, s, 0, keepdims=False)
    place = lax.dynamic_index_in_dim(positions, s, 0, keepdims=False)
    grad = lax.dynamic_index_in_dim(cotangent, s, 0, keepdims=False)
    tables = rotation(place)
    mask = allowed(x.shape[0])
    x = roll_features(x, row)
    kept, outs = [], []
    for layer in range(2):
        x, state = layer_forward(x, tables, weights[layer], mask)
        kept.append(state)
        outs.append(x)
    grad = roll_features(grad, row)
    grads, parts, gain_parts = [None, None], [None, None], [None, None]
    for layer in (1, 0):
        grad, attn, ffn, gain_grads = layer_backward(
            kept[layer], grad, tables, weights[layer], mask
        )
        grads[layer] = grad
        ffn = reduce_grads(ffn[0], ffn[1])
        attn = reduce_grads(attn[0], attn[1])
        parts[layer] = (attn, ffn)
        gain_parts[layer] = gain_grads

    def swap_out(arrays):
        n = lax.axis_size("row")
        keep = jnp.where(s == 0, arrays[0], arrays[1])
        got = mate(jnp.where(s == 0, arrays[1], arrays[0]), "section", 1)
        return jnp.where(s == 0, jnp.stack([keep, got]), jnp.stack([got, keep]))

    acts = roll_features(swap_out(outs), -row)[None]
    in_grads = roll_features(swap_out(grads), -row)[None]
    attn = swap_out([parts[0][0], parts[1][0]])
    ffn = swap_out([parts[0][1], parts[1][1]])

    def pick(array, start, width):
        return jnp.concatenate(
            [array[0, :, start : start + width], array[1, :, start : start + width]], 1
        )[None]

    gains = reduce_gains(jnp.stack(list(gain_parts[0]) + list(gain_parts[1])))
    return (
        acts,
        in_grads,
        pick(attn, 0, half_q),
        pick(attn, half_q, half_kv),
        pick(attn, half_q + half_kv, half_kv),
        pick(attn, half_q + 2 * half_kv, half_q),
        pick(ffn, 0, half_ff),
        pick(ffn, half_ff, half_ff),
        pick(ffn, 2 * half_ff, half_ff),
        gains[0:1],
        gains[1:2],
    )


def solution(mesh):
    placed = (
        P(None, "row", None),
        P(None, "row"),
        *[P("section", "row", "col")] * 7,
        *[P("section", "row")] * 2,
        P(None, "row", None),
    )
    return jax.shard_map(
        body,
        mesh=mesh,
        in_specs=placed,
        out_specs=(
            *[P("section", None, "row", None)] * 2,
            *[P("section", "row", "col")] * 7,
            *[P("section", "row")] * 2,
        ),
        check_vma=False,
    )
```

```python
import functools
import math

import jax
import jax.numpy as jnp
from jax import lax
from jax.experimental import pallas as pl
from jax.experimental.pallas import tpu as pltpu
from jax.sharding import PartitionSpec as P

HEAD_SIZE = 96
HALF = HEAD_SIZE // 2
EPSILON = 1e-05
ROPE_BASE = 100000.0
MASKED = -1e30
COST = 2 * 10**11
BF = jnp.bfloat16
F32 = jnp.float32
WHOLE = pl.BlockSpec(memory_space=pltpu.VMEM)
ANYWHERE = pl.BlockSpec(memory_space=pl.ANY)
FAR = pl.BlockSpec(memory_space=pltpu.HBM)
SCALAR = pl.BlockSpec(memory_space=pltpu.SMEM)


def mate(x, axis, k):
    n = lax.axis_size(axis)
    return lax.ppermute(x, axis, [(j, j ^ k) for j in range(n)])


def ring(x, by):
    n = lax.axis_size("row")
    return lax.ppermute(x, "row", [(j, (j + by) % n) for j in range(n)])


def gather_pieces(local):
    return [local] + [mate(local, "col", k) for k in range(1, lax.axis_size("col"))]


def dot(left, right):
    return jnp.dot(left, right, preferred_element_type=F32)


def dot_t(left, right):
    return lax.dot_general(left, right, (((1,), (1,)), ((), ())), preferred_element_type=F32)


def t_dot(left, right):
    return lax.dot_general(left, right, (((0,), (0,)), ((), ())), preferred_element_type=F32)


def stacked(refs):
    return jnp.concatenate([r[...] for r in refs], axis=0)


def kernel(name, body, ins, outs, grid=(), scratch=(), after=(), vmem=44, flops=0, path=False):
    arrays, specs, sizes = [], [], []
    for group in ins:
        sizes.append(len(group))
        for array, spec in group:
            arrays.append(array)
            specs.append(spec)
    count = len(arrays)
    after = list(after)
    arrays += after
    specs += [ANYWHERE] * len(after)

    def run(*refs):
        groups, at = [], 0
        for size in sizes:
            groups.append(refs[at : at + size])
            at += size
        at = count + len(after)
        body(*groups, refs[at : at + len(outs)], refs[at + len(outs) :])

    size = sum(a.size * a.dtype.itemsize for a in arrays[:count])
    size += sum(math.prod(o.shape) * jnp.dtype(o.dtype).itemsize for o, _ in outs)
    return pl.pallas_call(
        run,
        grid=grid,
        in_specs=specs,
        out_specs=[spec for _, spec in outs],
        out_shape=[shape for shape, _ in outs],
        scratch_shapes=list(scratch),
        compiler_params=pltpu.CompilerParams(vmem_limit_bytes=vmem << 20),
        cost_estimate=pl.CostEstimate(
            flops=COST if path else 0, bytes_accessed=size if path else 1, transcendentals=0
        ),
        name=name,
    )(*arrays)


def kernel_list(*args, **settings):
    return list(kernel(*args, **settings))


def shaped(shape, dtype=BF, spec=WHOLE):
    return (jax.ShapeDtypeStruct(tuple(shape), dtype), spec)


def full(arrays, spec=WHOLE):
    return [(a, spec) for a in arrays]


def enter(x, order, c, count, after=(), path=False):
    rows = x.shape[0] // count

    def body(xs, orders, cs, outs, _):
        for k in range(count):
            start = pl.multiple_of((cs[0][0] ^ k) * rows, 16)
            outs[k][...] = dot(xs[0][pl.ds(start, rows), :], orders[0][...]).astype(BF)

    return kernel_list(
        "enter",
        body,
        [full([x]), full([order]), full([c], SCALAR)],
        [shaped((rows, x.shape[1]))] * count,
        after=after,
        vmem=16,
        path=path,
    )


def leave(pieces, back, c, after=()):
    rows, width = pieces[0].shape
    count = len(pieces)

    def body(ps, orders, cs, outs, _):
        y = dot(stacked(ps), orders[0][...]).astype(BF)
        for k in range(count):
            start = pl.multiple_of((cs[0][0] ^ k) * rows, 16)
            outs[0][pl.ds(start, rows), :] = y[k * rows : (k + 1) * rows]

    return kernel(
        "leave",
        body,
        [full(pieces), full([back]), full([c], SCALAR)],
        [shaped((rows * count, width))],
        after=after,
        vmem=20,
        flops=2 * rows * count * width * width,
    )[0]


def pack(parts, s, after=()):
    h = parts[0].shape[0] // 2
    width = sum(p.shape[1] for p in parts)

    def body(ps, ss, outs, _):
        for out, side in zip(outs, (ss[0][0], 1 - ss[0][0])):
            start = pl.multiple_of(side * h, 16)
            at = 0
            for p in ps:
                out[:, at : at + p.shape[1]] = p[pl.ds(start, h), :]
                at += p.shape[1]

    return kernel("pack", body, [full(parts), full([s], SCALAR)], [shaped((h, width))] * 2, after=after, vmem=16)


def unpack(mine, theirs, s, widths, after=()):
    h, total = mine[0].shape

    def body(ms, ts, ss, outs, scratch):
        side = ss[0][0]
        for layer in range(2):

            @pl.when(side == layer)
            def _():
                copies = [
                    pltpu.make_async_copy(ref, scratch[k], scratch[2].at[k])
                    for k, ref in enumerate((ms[layer], ts[layer]))
                ]
                for copy in copies:
                    copy.start()
                for copy in copies:
                    copy.wait()

        for k, at in enumerate((side, 1 - side)):
            start = pl.multiple_of(at * h, 16)
            column = 0
            for out in outs:
                width = out.shape[1]
                out[pl.ds(start, h), :] = scratch[k][:, column : column + width].astype(F32)
                column += width

    return kernel(
        "unpack",
        body,
        [full(mine, FAR), full(theirs, FAR), full([s], SCALAR)],
        [shaped((2 * h, w), F32) for w in widths],
        scratch=[pltpu.VMEM((h, total), BF)] * 2 + [pltpu.SemaphoreType.DMA((2,))],
        after=after,
        vmem=20,
    )


def place_out(mine, theirs, s, after=()):
    shape = mine[0].shape

    def body(ms, ts, ss, outs, scratch):
        side = ss[0][0]
        for layer in range(2):

            @pl.when(side == layer)
            def _():
                copies = [
                    pltpu.make_async_copy(ref, outs[0].at[at], scratch[0].at[k])
                    for k, (ref, at) in enumerate(((ms[layer], layer), (ts[layer], 1 - layer)))
                ]
                for copy in copies:
                    copy.start()
                for copy in copies:
                    copy.wait()

    return kernel(
        "place_out",
        body,
        [full(mine, FAR), full(theirs, FAR), full([s], SCALAR)],
        [shaped((2,) + shape, mine[0].dtype)],
        scratch=[pltpu.SemaphoreType.DMA((2,))],
        after=after,
        vmem=16,
    )[0]


def meet(after):
    def body(outs, _):
        outs[0][...] = jnp.zeros(outs[0].shape, F32)

    return kernel_list("meet", body, [], [shaped((8, 128), F32)], after=after, vmem=2, path=True)


def turn(x, cosine, sine, swap, sign):
    high = x.astype(BF)
    low = (x - high.astype(F32)).astype(BF)
    return x * cosine + (dot(high, swap) + dot(low, swap)) * (sine * sign)


class Fetch:
    def __init__(self, slots, target, sems, column, base=0):
        h, width = slots[0].shape[0], target.shape[1]
        self.target = target
        self.copies = [
            pltpu.make_async_copy(
                ref.at[:, pl.ds(column, width)], target.at[pl.ds(k * h, h), :], sems.at[base + k]
            )
            for k, ref in enumerate(slots)
        ]
        for copy in self.copies:
            copy.start()

    def get(self):
        for copy in self.copies:
            copy.wait()
        return self.target[...]


def pieces_of(value, outs, count, first=0):
    rows = value.shape[0] // count
    for k in range(count):
        outs[first + k][...] = value[k * rows : (k + 1) * rows]


def project(pieces, gain, slots, tables, swaps, width_q, after=()):
    rows, width = pieces[0].shape
    tokens = rows * len(pieces)

    def body(ps, gains, ws, ts, ks, outs, scratch):
        w = Fetch(ws, scratch[0], scratch[1], 0)
        x = stacked(ps).astype(F32)
        scale = lax.rsqrt(jnp.mean(x * x, axis=-1, keepdims=True) + EPSILON)
        n1 = (x * scale * gains[0][...]).astype(BF)
        outs[0][...] = n1
        w.get()
        for part in range(2):
            cols = slice(part * width_q, (part + 1) * width_q)
            raw = dot(n1, scratch[0][:, cols])
            turned = turn(raw, ts[0][:, cols], ts[1][:, cols], ks[part][...], 1.0)
            outs[1 + part][...] = turned.astype(BF)

    return kernel(
        "project",
        body,
        [full(pieces), full([gain]), full(slots, FAR), full(tables), full(swaps)],
        [shaped((tokens, width)), shaped((tokens, width_q)), shaped((tokens, width_q))],
        scratch=[pltpu.VMEM((width, 2 * width_q), BF), pltpu.SemaphoreType.DMA((len(slots),))],
        path=True,
        after=after,
        vmem=24,
        flops=4 * tokens * width * width_q,
    )


def head(ref, at):
    return ref[:, at * HEAD_SIZE : (at + 1) * HEAD_SIZE]


def attention(query, own, there, orders, slots, count, after=()):
    tokens, width_q = query.shape
    rows = tokens // count
    width = slots[0].shape[0] * len(slots)
    heads = width_q // HEAD_SIZE
    kv = heads // 2
    scale = 1.0 / math.sqrt(HEAD_SIZE)

    def body(qs, owns, theres, os, ws, outs, scratch):
        w = Fetch(ws, scratch[0], scratch[1], 2 * width_q)
        seen = os[1][...] <= os[0][...]
        for g in range(kv):
            keys = jnp.concatenate([head(owns[0], g), head(theres[0], g)], 0)
            values = jnp.concatenate([head(owns[0], kv + g), head(theres[0], kv + g)], 0)
            for h in range(2 * g, 2 * g + 2):
                scores = jnp.where(seen, dot_t(keys, head(qs[0], h)), MASKED)
                peak = jnp.max(scores, axis=0, keepdims=True)
                weights = jnp.exp((scores - peak) * scale)
                total = jnp.sum(weights, axis=0, keepdims=True)
                outs[1][h : h + 1, :] = peak * scale + jnp.log(total)
                mixed = t_dot(values, weights.astype(BF)) / total
                outs[0][:, h * HEAD_SIZE : (h + 1) * HEAD_SIZE] = mixed.T.astype(BF)
        pieces_of(dot_t(outs[0][...], w.get()).astype(BF), outs, count, 2)

    mixed, log_sums, *pieces = kernel(
        "attention",
        body,
        [full([query]), full([own]), full([there]), full(orders), full(slots, FAR)],
        [shaped((tokens, width_q)), shaped((heads, tokens), F32)] + [shaped((rows, width))] * count,
        scratch=[pltpu.VMEM((width, width_q), BF), pltpu.SemaphoreType.DMA((len(slots),))],
        path=True,
        after=after,
        vmem=30,
        flops=2 * tokens * width * width_q + 8 * tokens * tokens * width_q,
    )
    return mixed, log_sums, pieces


def attention_back(pieces, query, own, there, log_sums, orders, slots, after=()):
    tokens, width_q = query.shape
    width = slots[0].shape[0] * len(slots)
    heads = width_q // HEAD_SIZE
    kv = heads // 2
    scale = 1.0 / math.sqrt(HEAD_SIZE)

    def body(ps, qs, owns, theres, ls, os, ws, outs, scratch):
        w = Fetch(ws, scratch[0], scratch[1], 2 * width_q)
        seen = os[1][...] <= os[0][...]
        scratch[2][...] = dot(stacked(ps), w.get()).astype(BF)
        for g in range(kv):
            keys = jnp.concatenate([head(owns[0], g), head(theres[0], g)], 0)
            values = jnp.concatenate([head(owns[0], kv + g), head(theres[0], kv + g)], 0)
            sums = [None, None]
            for h in range(2 * g, 2 * g + 2):
                q, grad = head(qs[0], h), head(scratch[2], h)
                scores = dot_t(keys, q) * scale - ls[0][h : h + 1, :]
                probs = jnp.exp(jnp.where(seen, scores, MASKED))
                grad_probs = dot_t(values, grad)
                inner = jnp.sum(probs * grad_probs, axis=0, keepdims=True)
                grad_scores = (probs * (grad_probs - inner)).astype(BF)
                cols = slice(h * HEAD_SIZE, (h + 1) * HEAD_SIZE)
                outs[0][:, cols] = (t_dot(keys, grad_scores) * scale).T
                terms = (dot(grad_scores, q) * scale, dot(probs.astype(BF), grad))
                sums = [t if u is None else t + u for t, u in zip(terms, sums)]
            for at, total in zip((g, kv + g), sums):
                cols = slice(at * HEAD_SIZE, (at + 1) * HEAD_SIZE)
                outs[1][:, cols] = total[:tokens]
                outs[2][:, cols] = total[tokens:].astype(BF)

    return kernel(
        "attention_back",
        body,
        [full(pieces), full([query]), full([own]), full([there]), full([log_sums])]
        + [full(orders), full(slots, FAR)],
        [shaped((tokens, width_q), F32)] * 2 + [shaped((tokens, width_q))],
        scratch=[
            pltpu.VMEM((width, width_q), BF),
            pltpu.SemaphoreType.DMA((len(slots),)),
            pltpu.VMEM((tokens, width_q), BF),
        ],
        path=True,
        after=after,
        vmem=32,
        flops=2 * tokens * width * width_q + 20 * tokens * tokens * width_q,
    )


def project_back(grad_query, grad_own, grad_there, slots, tables, swaps, count, after=()):
    tokens, width_q = grad_query.shape
    rows = tokens // count
    width = slots[0].shape[0] * len(slots)

    def body(qs, owns, theres, ws, ts, ks, outs, scratch):
        w = Fetch(ws, scratch[0], scratch[1], 0)
        grads = (qs[0][...], owns[0][...] + theres[0][...].astype(F32))
        for part in range(2):
            cols = slice(part * width_q, (part + 1) * width_q)
            turned = turn(grads[part], ts[0][:, cols], ts[1][:, cols], ks[part][...], -1.0)
            outs[count][:, cols] = turned.astype(BF)
        pieces_of(dot_t(outs[count][...], w.get()).astype(BF), outs, count)

    *pieces, grads = kernel(
        "project_back",
        body,
        [full([grad_query]), full([grad_own]), full([grad_there]), full(slots, FAR)]
        + [full(tables), full(swaps)],
        [shaped((rows, width))] * count + [shaped((tokens, 2 * width_q))],
        scratch=[pltpu.VMEM((width, 2 * width_q), BF), pltpu.SemaphoreType.DMA((len(slots),))],
        path=True,
        after=after,
        vmem=24,
        flops=4 * tokens * width * width_q,
    )
    return pieces, grads


def feed_forward(pieces, slots, after=()):
    rows, width = pieces[0].shape
    count = len(pieces)
    tokens = rows * count
    units = slots[0].shape[1] // 3

    def body(ps, ws, outs, scratch):
        parts = [
            Fetch(ws, scratch[k], scratch[3], k * units, k * len(slots)) for k in range(3)
        ]
        n2 = stacked(ps)
        gate = dot(n2, parts[0].get())
        up = dot(n2, parts[1].get())
        outs[0][...] = gate.astype(BF)
        outs[1][...] = up.astype(BF)
        outs[2][...] = (gate / (1.0 + jnp.exp(-gate)) * up).astype(BF)
        pieces_of(dot_t(outs[2][...], parts[2].get()).astype(BF), outs, count, 3)

    gate, up, hidden, *out = kernel(
        "feed_forward",
        body,
        [full(pieces), full(slots, FAR)],
        [shaped((tokens, units))] * 3 + [shaped((rows, width))] * count,
        scratch=[pltpu.VMEM((width, units), BF)] * 3
        + [pltpu.SemaphoreType.DMA((3 * len(slots),))],
        path=True,
        after=after,
        vmem=32,
        flops=6 * tokens * width * units,
    )
    return gate, up, hidden, out


def feed_forward_back(pieces, gate, up, slots, after=()):
    rows, width = pieces[0].shape
    count = len(pieces)
    tokens = rows * count
    units = gate.shape[1]

    def body(ps, gus, ws, outs, scratch):
        down = Fetch(ws, scratch[0], scratch[2], 2 * units)
        rest = Fetch(ws, scratch[1], scratch[2], 0, len(slots))
        grad = dot(stacked(ps), down.get())
        gate, up = gus[0][...].astype(F32), gus[1][...].astype(F32)
        sig = 1.0 / (1.0 + jnp.exp(-gate))
        part = grad * sig
        outs[0][:, :units] = (part * up * (1.0 + gate * (1.0 - sig))).astype(BF)
        outs[0][:, units:] = (part * gate).astype(BF)
        pieces_of(dot_t(outs[0][...], rest.get()).astype(BF), outs, count, 1)

    grads, *out = kernel(
        "feed_forward_back",
        body,
        [full(pieces), full([gate, up]), full(slots, FAR)],
        [shaped((tokens, 2 * units))] + [shaped((rows, width))] * count,
        scratch=[pltpu.VMEM((width, units), BF), pltpu.VMEM((width, 2 * units), BF)]
        + [pltpu.SemaphoreType.DMA((2 * len(slots),))],
        path=True,
        after=after,
        vmem=32,
        flops=6 * tokens * width * units,
    )
    return grads, out


def weight_grads(terms, half, block, got=None, after=()):
    width = terms[0][0][0].shape[1] // 2
    tokens = terms[0][1].shape[0]
    steps = [rhs.shape[1] // block for _, rhs in terms]
    total = sum(rhs.shape[1] for _, rhs in terms)
    n = 1 if got is None else lax.axis_size("row")
    rows = width // n
    ins, begins = [], []
    for k, (lhs, rhs) in enumerate(terms):
        begin = sum(steps[:k])
        begins.append(begin)
        ins.append([(a, pl.BlockSpec((a.shape[0], width), lambda j: (0, half))) for a in lhs])
        place = functools.partial(
            lambda j, lo, hi: (0, jnp.clip(j - lo, 0, hi)), lo=begin, hi=steps[k] - 1
        )
        ins.append([(rhs, pl.BlockSpec((tokens, block), place))])
    ins.append([] if got is None else [(got, pl.BlockSpec((width, block), lambda j: (0, j)))])

    def body(*refs):
        *refs, more, outs, scratch = refs
        j = pl.program_id(0)
        for k, begin in enumerate(begins):
            lhs, rhs = refs[2 * k : 2 * k + 2]

            @pl.when(j == begin)
            def _():
                scratch[0][...] = stacked(lhs).T

            @pl.when((j >= begin) & (j < begin + steps[k]))
            def _():
                value = dot(scratch[0][...], rhs[0][...])
                if got is not None:
                    value = value + more[0][...].astype(F32)
                value = value.astype(BF)
                for k in range(n):
                    outs[k][...] = value[k * rows : (k + 1) * rows]

    out = kernel(
        "weight_grads",
        body,
        ins,
        [shaped((rows, total), BF, pl.BlockSpec((rows, block), lambda j: (0, j)))] * n,
        grid=(sum(steps),),
        scratch=[pltpu.VMEM((width, tokens), BF)],
        after=after,
        vmem=20,
        flops=2 * tokens * width * total,
    )
    return out[0] if got is None else out


def total_of(refs):
    total = refs[0][...].astype(F32)
    for r in refs[1:]:
        total = total + r[...].astype(F32)
    return total


def inverse_rms(x):
    return lax.rsqrt(jnp.mean(x * x, axis=-1, keepdims=True) + EPSILON)


def add_and_norm(x, terms, gain, after=()):
    def body(xs, ts, gains, outs, _):
        middle = xs[0][...].astype(F32) + total_of(ts)
        outs[0][...] = middle
        outs[1][...] = (middle * inverse_rms(middle) * gains[0][...]).astype(BF)

    return kernel(
        "add_and_norm",
        body,
        [full([x]), full(terms), full([gain])],
        [shaped(x.shape, F32), shaped(x.shape)],
        path=True,
        after=after,
        vmem=16,
    )


def add_up(middle, terms, after=()):
    def body(xs, ts, outs, _):
        outs[0][...] = (xs[0][...] + total_of(ts)).astype(BF)

    return kernel(
        "add_up",
        body,
        [full([middle]), full(terms)],
        [shaped(middle.shape)],
        after=after,
        vmem=16,
        path=True,
    )[0]


def norm_back(x, terms, gain, straight, after=()):
    def body(xs, ts, gains, ss, outs, _):
        x = xs[0][...].astype(F32)
        grad = total_of(ts)
        scale = inverse_rms(x)
        unit = x * scale
        scaled = grad * gains[0][...]
        outs[0][...] = jnp.sum(grad * unit, axis=0, keepdims=True)
        mean = jnp.mean(scaled * unit, axis=-1, keepdims=True)
        total = ss[0][...].astype(F32) + scale * (scaled - unit * mean)
        outs[1][...] = total
        outs[2][...] = total.astype(BF)

    return kernel(
        "norm_back",
        body,
        [full([x]), full(terms), full([gain]), full([straight])],
        [shaped((1, x.shape[1]), F32), shaped(x.shape, F32), shaped(x.shape)],
        path=True,
        after=after,
        vmem=16,
    )


def behind(value, *others):
    return lax.optimization_barrier((value, *others))[0]


def strides(count):
    return [count * (k + 1) // 3 - count * k // 3 for k in range(3)]


class Gather:
    def __init__(self, mine):
        self.slots = [mine]
        self.others = [mate(mine, "section", 1)]
        self.parts = strides(lax.axis_size("row") - 1)

    def hop(self, *now):
        if now:
            self.slots[-1] = behind(self.slots[-1], *now)
        for _ in range(self.parts.pop(0)):
            self.slots.append(ring(self.slots[-1], -1))
            self.others.append(mate(self.slots[-1], "section", 1))
        return [self.slots[-1]]

    def all(self):
        return self.slots + self.others


class Scatter:
    def __init__(self, slots):
        self.slots = list(slots)
        self.moving = self.slots.pop()
        self.parts = strides(len(slots) - 1)

    def hop(self, *now):
        self.moving = behind(self.moving, *now)
        for _ in range(self.parts.pop(0)):
            got = ring(self.moving, 1).astype(F32)
            self.moving = (self.slots.pop().astype(F32) + got).astype(BF)
        return [self.moving]


def received(pieces):
    return [pieces[0]] + [mate(pieces[k], "col", k) for k in range(1, len(pieces))]


def feature_order(width, s):
    n = lax.axis_size("row")
    i = lax.axis_index("row")
    h = width // (2 * n)
    place = jnp.arange(width)
    part, block, inner = place // (n * h), (place // h) % n, place % h
    source = ((i + block) % n) * 2 * h + ((s + part) % 2) * h + inner
    return (place[:, None] == source[None, :]).astype(BF), (
        source[:, None] == place[None, :]
    ).astype(BF)


def swap_matrix(width, turned):
    source, place = jnp.arange(width)[:, None], jnp.arange(width)[None, :]
    first = (place % HEAD_SIZE) < HALF
    hit = jnp.where(first, source == place + HALF, source == place - HALF) & (place < turned)
    return jnp.where(hit, jnp.where(first, -1.0, 1.0), 0.0).astype(BF)


def token_tables(place, width_q, width_kv):
    power = -(jnp.arange(HALF, dtype=F32) * 2.0) / HEAD_SIZE
    angles = place.astype(F32)[:, None] * (ROPE_BASE**power)[None, :]
    lane = jnp.arange(2 * width_q)
    turned = lane < width_q + width_kv
    spread = (jnp.arange(HALF)[:, None] == (lane % HALF)[None, :]) & turned[None, :]
    rest = jnp.where(turned, 0.0, 1.0).astype(F32)[None, :]
    return spread_tables(jnp.cos(angles), jnp.sin(angles), spread.astype(BF), rest)


def spread_tables(cosine, sine, spread, rest):
    def body(ts, ms, rs, outs, _):
        for k in range(2):
            left, total = ts[k][...], jnp.zeros(outs[k].shape, F32)
            for _ in range(3):
                part = left.astype(BF)
                total = total + dot(part, ms[0][...])
                left = left - part.astype(F32)
            outs[k][...] = total + rs[0][...] if k == 0 else total

    shape = (cosine.shape[0], spread.shape[1])
    return kernel(
        "spread_tables",
        body,
        [full([cosine, sine]), full([spread]), full([rest])],
        [shaped(shape, F32)] * 2,
        vmem=16,
    )


def reduce_gains(gains):
    s = lax.axis_index("section")
    n = lax.axis_size("row")
    total = gains
    for k in range(1, lax.axis_size("col")):
        total = total + mate(gains, "col", k)
    h = gains.shape[1] // (2 * n)
    total = total.reshape(4, 2, n, h)
    first, second = total[:, 0], total[:, 1]
    total = jnp.concatenate(
        [jnp.where(s == 0, first, second), jnp.where(s == 0, second, first)], -1
    )
    here = total[:, 0]
    for k in range(1, n):
        here = here + ring(total[:, k], k)
    keep = jnp.where(s == 0, here[:2], here[2:])
    send = jnp.where(s == 0, here[2:], here[:2])
    return keep + mate(send, "section", 1)


def body(
    inputs,
    positions,
    w_query,
    key_weight,
    value_weight,
    w_out,
    w_gate,
    w_up,
    w_down,
    gain_attn,
    gain_ffn,
    cotangent,
):
    s = lax.axis_index("section")
    c = lax.axis_index("col")
    n = lax.axis_size("row")
    count = lax.axis_size("col")
    width_q, width_kv, units = w_query.shape[2], key_weight.shape[2], w_gate.shape[2]
    tokens, width = inputs.shape[1:]
    rows = tokens // count
    s_here, c_here = s.astype(jnp.int32)[None], c.astype(jnp.int32)[None]

    def start(parts, after):
        keep, send = pack([p[0] for p in parts], s_here, after)
        got = mate(send, "section", 1)
        return [jnp.where(s == layer, keep, got) for layer in range(2)]

    attn_start = start((w_query, key_weight, value_weight, w_out), [])
    first = attn_start[0]
    a = Gather(first)
    come = a.hop()
    ffn_start = start((w_gate, w_up, w_down), [first])
    f = Gather(ffn_start[0])

    gains = behind(jnp.concatenate([gain_attn, gain_ffn], 0), first)
    pair = mate(gains, "section", 1)
    gains = jnp.concatenate([jnp.where(s == 0, gains, pair), jnp.where(s == 0, pair, gains)], 0)
    gains = jnp.stack([gains] + [ring(gains, -k) for k in range(1, n)], 1)
    gains = gains.reshape(4, n, 2, -1)
    gains = jnp.where(s == 0, gains, gains[:, :, ::-1]).transpose(0, 2, 1, 3).reshape(4, 1, -1)
    gains = gains.astype(F32)

    inputs, positions = behind(inputs, first), behind(positions, *come)
    order, back_order = feature_order(width, behind(s, *come))
    swaps = [swap_matrix(width_q, width_q), swap_matrix(width_q, width_kv)]
    x = lax.dynamic_index_in_dim(inputs, s, 0, keepdims=False)
    place = lax.dynamic_index_in_dim(positions, s, 0, keepdims=False)
    cot = lax.dynamic_index_in_dim(cotangent, s, 0, keepdims=False)
    piece = jnp.arange(count) ^ c
    token = (piece[:, None] * rows + jnp.arange(rows)[None, :]).reshape(-1)
    place = jnp.concatenate(
        [lax.dynamic_slice_in_dim(place, (c ^ k) * rows, rows) for k in range(count)]
    )
    tables = token_tables(place, width_q, width_kv)
    parity = lax.axis_index("row") % 2

    def order_of(side):
        half = tokens // 2
        return token + jnp.where(side == 0, jnp.where(token < half, 0, 2 * half), half)

    own_order = order_of(parity)
    orders = [own_order[None, :], jnp.concatenate([own_order, order_of(1 - parity)])[:, None]]

    point = meet(come)
    come = f.hop(*come)
    x = enter(x, order, c_here, count, a.hop() + come + point, True)
    a.hop()
    grad = enter(cot, order, c_here, count)

    kept, outs, gathers = [], [], []
    for layer in range(2):
        gain1, gain2 = gains[2 * layer], gains[2 * layer + 1]
        last = layer == 1
        gathers.append((a, f))
        come = meet(x[1:] + a.slots[-1:] + grad[:1]) if last else []
        n1, query, own = project(x, gain1, a.all(), tables, swaps, width_q, come)
        there = mate(own, "row", 1)
        come = f.hop(there)
        mixed, sums, y = attention(query, own, there, orders, a.all(), count)
        sent = received(y)
        f.hop(sent[-1])
        if not last:
            a, f_old = Gather(attn_start[1]), f
            a.hop(sent[-1])
        middle, n2 = add_and_norm(x[0], sent, gain2, come)
        n2 = gather_pieces(n2)
        point = meet(n2[1:] + f.slots[-1:] + a.slots[-1:])
        if not last:
            f = Gather(ffn_start[1])
            come = f.hop(n2[-1]) + a.hop(n2[-1])
        gate, up, hidden, y = feed_forward(n2, gathers[-1][1].all(), point)
        kept.append((x[0], n1, query, own, there, mixed, sums, middle, n2, gate, up, hidden))
        if not last:
            sent = received(y)
            a.hop(sent[-1])
            x = gather_pieces(add_up(middle, sent, come))
            outs.append(x)

    def to_owner(value, layer):
        return lax.ppermute(value, "section", [(1 - layer, layer)])

    left, parts, gain_parts = [None, None], [None, None], [None, None]
    last_y, s_a, come = y, None, []
    for layer in (1, 0):
        a, f = gathers[layer]
        x, n1, query, own, there, mixed, sums, middle, n2, gate, up, hidden = kept[layer]
        gain1, gain2 = gains[2 * layer], gains[2 * layer + 1]
        grad_gu, y = feed_forward_back(grad, gate, up, f.all(), come)
        come = s_a.hop(grad[-1]) if s_a else []
        sent = received(y)
        down, rest = [(grad, behind(hidden, grad_gu))], [(n2, grad_gu)]
        got = mate(weight_grads(down, 1, units // 2), "section", 1)
        s_d = Scatter(weight_grads(down, 0, units // 2, got))
        other = weight_grads(rest, 1, units // 2)
        got = mate(other, "section", 1)
        come += [s_d.moving, other]
        g_gain2, grad_middle, grad_attn = norm_back(middle, sent, gain2, grad[0], come)
        come = s_d.hop(sent[-1]) + (s_a.hop(sent[-1]) if s_a else [])
        s_f = Scatter(weight_grads(rest, 0, units // 2, behind(got, grad_attn)))
        grad_attn = gather_pieces(grad_attn)
        grad_query, grad_own, grad_there = attention_back(
            grad_attn, query, own, there, sums, orders, a.all(), come + [s_f.moving]
        )
        come = s_f.hop(grad_attn[-1])
        if layer == 1:
            last_y = received([behind(p, grad_attn[-1]) for p in last_y])
            left[0] = leave([behind(p, grad_there) for p in outs[0]], back_order, c_here)
            come += last_y[1:] + [left[0]]
        else:
            last_y = add_up(kept[1][7], last_y)
            outs.append(gather_pieces(behind(last_y, grad_attn[-1])))
            left[1] = leave([behind(p, grad_there) for p in grad], back_order, c_here)
            come += outs[1][1:] + [left[1]]
        back = mate(grad_there, "row", 1)
        y, grad_qkv = project_back(
            grad_query, grad_own, back, a.all(), tables, swaps, count, come
        )
        come = s_f.hop(back) + (s_a.hop(back) if s_a else s_d.hop(back))
        sent = received(y)
        terms = [([n1], grad_qkv), (grad_attn, mixed)]
        other = weight_grads(terms, 1, width_q)
        got = mate(other, "section", 1)
        mine = weight_grads(terms, 0, width_q, got)
        came = come + list(mine[:1] if layer == 0 else [other])
        g_gain1, _, grad = norm_back(x, sent, gain1, grad_middle, came)
        come = s_f.hop(sent[-1]) + s_d.hop(sent[-1])
        s_a = Scatter(mine)
        grad = gather_pieces(grad)
        if layer == 1:
            come += [s_a.moving]
        parts[layer] = (s_a, s_f, s_d)
        gain_parts[layer] = (g_gain1, g_gain2)

    come += s_a.hop(sent[-1])
    acts = [left[0], leave([behind(p, g_gain1) for p in outs[1]], back_order, c_here)]
    point = meet(grad[1:] + acts[1:])
    grads = [leave([behind(p, *point) for p in grad], back_order, c_here), left[1]]
    grads_there = [to_owner(v, k) for k, v in enumerate(grads)]
    acts_there = [to_owner(behind(v, *point), k) for k, v in enumerate(acts)]
    gain_grads = jnp.concatenate(list(gain_parts[0]) + list(gain_parts[1]), 0)
    gain_grads = reduce_gains(behind(gain_grads, *point))
    come = s_d.hop(*come) + s_a.hop(*come)
    point = meet(come + grads_there + acts_there)
    s_a.hop(*come)
    acts = place_out(acts, acts_there, s_here, point)
    grads = place_out(grads, grads_there, s_here, point)

    def owned(k, widths):
        values = [behind(p[k].moving, *come) if k else p[k].moving for p in parts]
        return unpack(values, [to_owner(v, layer) for layer, v in enumerate(values)], s_here, widths)

    (g_down,) = owned(2, (units,))
    g_gate, g_up = owned(1, (units, units))
    g_query, g_key, g_value, g_out = owned(0, (width_q, width_kv, width_kv, width_q))
    return (
        acts[None],
        grads[None],
        *[g[None] for g in (g_query, g_key, g_value, g_out, g_gate, g_up, g_down)],
        gain_grads[0:1],
        gain_grads[1:2],
    )


def solution(mesh):
    placed = (
        P(None, "row", None),
        P(None, "row"),
        *[P("section", "row", "col")] * 7,
        *[P("section", "row")] * 2,
        P(None, "row", None),
    )
    return jax.shard_map(
        body,
        mesh=mesh,
        in_specs=placed,
        out_specs=(
            *[P("section", None, "row", None)] * 2,
            *[P("section", "row", "col")] * 7,
            *[P("section", "row")] * 2,
        ),
        check_vma=False,
    )
```

```python
import functools
import math

import jax
import jax.numpy as jnp
from jax import lax
from jax.experimental import pallas as pl
from jax.experimental.pallas import tpu as pltpu
from jax.sharding import PartitionSpec as P

HEAD_SIZE = 96
HALF = HEAD_SIZE // 2
EPSILON = 1e-05
ROPE_BASE = 100000.0
MASKED = -1e30
COST = 60000000000
COSTS = {'add_slots': 3000000000, 'choose': 2000000000, 'sum_gains': 1000000000, 'own_gains': 1000000000}
BF = jnp.bfloat16
F32 = jnp.float32
WHOLE = pl.BlockSpec(memory_space=pltpu.VMEM)
ANYWHERE = pl.BlockSpec(memory_space=pl.ANY)
FAR = pl.BlockSpec(memory_space=pltpu.HBM)
FETCHED = object()
SCALAR = pl.BlockSpec(memory_space=pltpu.SMEM)


def mate(x, axis, k):
    n = lax.axis_size(axis)
    return lax.ppermute(x, axis, [(j, j ^ k) for j in range(n)])


def ring(x, by):
    n = lax.axis_size("row")
    return lax.ppermute(x, "row", [(j, (j + by) % n) for j in range(n)])


def gather_pieces(local):
    return [local] + [mate(local, "col", k) for k in range(1, lax.axis_size("col"))]


def dot(left, right):
    return jnp.dot(left, right, preferred_element_type=F32)


def dot_t(left, right):
    return lax.dot_general(left, right, (((1,), (1,)), ((), ())), preferred_element_type=F32)


def t_dot(left, right):
    return lax.dot_general(left, right, (((0,), (0,)), ((), ())), preferred_element_type=F32)


def stacked(refs):
    return jnp.concatenate([r[...] for r in refs], axis=0)


def kernel(name, body, ins, outs, grid=(), scratch=(), after=(), vmem=44, flops=0, path=False):
    arrays, specs, sizes, fetched = [], [], [], []
    for group in ins:
        sizes.append(len(group))
        for array, spec in group:
            if spec is FETCHED:
                fetched.append(len(arrays))
            arrays.append(array)
            specs.append(ANYWHERE if spec is FETCHED else spec)
    count = len(arrays)
    after = list(after)
    arrays += after
    specs += [ANYWHERE] * len(after)
    targets = [pltpu.VMEM(arrays[k].shape, arrays[k].dtype) for k in fetched]
    if fetched:
        targets.append(pltpu.SemaphoreType.DMA((len(fetched),)))

    def run(*refs):
        refs = list(refs)
        extra = refs[len(refs) - len(targets) :] if targets else []
        refs = refs[: len(refs) - len(targets)]
        copies = [
            pltpu.make_async_copy(refs[k], extra[j], extra[-1].at[j])
            for j, k in enumerate(fetched)
        ]
        for copy in copies:
            copy.start()
        for copy in copies:
            copy.wait()
        for j, k in enumerate(fetched):
            refs[k] = extra[j]
        groups, at = [], 0
        for size in sizes:
            groups.append(refs[at : at + size])
            at += size
        at = count + len(after)
        body(*groups, refs[at : at + len(outs)], refs[at + len(outs) :])

    size = sum(a.size * a.dtype.itemsize for a in arrays[:count])
    size += sum(math.prod(o.shape) * jnp.dtype(o.dtype).itemsize for o, _ in outs)
    return pl.pallas_call(
        run,
        grid=grid,
        in_specs=specs,
        out_specs=[spec for _, spec in outs],
        out_shape=[shape for shape, _ in outs],
        scratch_shapes=list(scratch) + targets,
        compiler_params=pltpu.CompilerParams(vmem_limit_bytes=vmem << 20),
        cost_estimate=pl.CostEstimate(
            flops=COST if path else COSTS.get(name, 0),
            bytes_accessed=size if path else 1,
            transcendentals=0,
        ),
        name=name,
    )(*arrays)


def kernel_list(*args, **settings):
    return list(kernel(*args, **settings))


def shaped(shape, dtype=BF, spec=WHOLE):
    return (jax.ShapeDtypeStruct(tuple(shape), dtype), spec)


def full(arrays, spec=WHOLE):
    return [(a, spec) for a in arrays]


def enter(x, order, c, count, after=(), path=False):
    rows = x.shape[0] // count

    def body(xs, orders, cs, outs, _):
        for k in range(count):
            start = pl.multiple_of((cs[0][0] ^ k) * rows, 16)
            outs[k][...] = dot(xs[0][pl.ds(start, rows), :], orders[0][...]).astype(BF)

    return kernel_list(
        "enter",
        body,
        [full([x], FETCHED), full([order], FETCHED), full([c], SCALAR)],
        [shaped((rows, x.shape[1]))] * count,
        after=after,
        vmem=16,
        path=path,
    )


def leave(pieces, back, c, after=(), path=False):
    rows, width = pieces[0].shape
    count = len(pieces)

    def body(ps, orders, cs, outs, _):
        y = dot(stacked(ps), orders[0][...]).astype(BF)
        for k in range(count):
            start = pl.multiple_of((cs[0][0] ^ k) * rows, 16)
            outs[0][pl.ds(start, rows), :] = y[k * rows : (k + 1) * rows]

    return kernel(
        "leave",
        body,
        [full(pieces), full([back]), full([c], SCALAR)],
        [shaped((rows * count, width))],
        after=after,
        vmem=20,
        path=path,
        flops=2 * rows * count * width * width,
    )[0]


def pack(parts, s, after=()):
    flips = [isinstance(p, tuple) for p in parts]
    parts = [p[0] if flip else p for p, flip in zip(parts, flips)]
    shapes = [p.shape[::-1] if flip else p.shape for p, flip in zip(parts, flips)]
    h = shapes[0][0] // 2
    width = sum(shape[1] for shape in shapes)

    def body(ps, ss, outs, scratch):
        scratch, sources = list(scratch), []
        for p, flip in zip(ps, flips):
            if flip:
                sources.append(scratch.pop(0))
                sources[-1][...] = p[...].T
            else:
                sources.append(p)
        for out, side in zip(outs, (ss[0][0], 1 - ss[0][0])):
            start = pl.multiple_of(side * h, 16)
            at = 0
            for p in sources:
                out[:, at : at + p.shape[1]] = p[pl.ds(start, h), :]
                at += p.shape[1]

    return kernel(
        "pack",
        body,
        [full(parts, FETCHED), full([s], SCALAR)],
        [shaped((h, width))] * 2,
        scratch=[pltpu.VMEM(shape, BF) for shape, flip in zip(shapes, flips) if flip],
        after=after,
        vmem=16,
    )


def unpack(mine, got, s, widths, after=(), flips=()):
    h, total = mine[0].shape

    def body(ms, gs, ss, outs, scratch):
        side = ss[0][0]
        for layer in range(2):

            @pl.when(side == layer)
            def _():
                copies = [
                    pltpu.make_async_copy(ref, scratch[k], scratch[2].at[k])
                    for k, ref in enumerate((ms[layer], gs[0]))
                ]
                for copy in copies:
                    copy.start()
                for copy in copies:
                    copy.wait()

        turned = list(scratch[3:])
        targets = [turned.pop(0) if k in flips else out for k, out in enumerate(outs)]
        for k, at in enumerate((side, 1 - side)):
            start = pl.multiple_of(at * h, 16)
            column = 0
            for target in targets:
                width = target.shape[1]
                target[pl.ds(start, h), :] = scratch[k][:, column : column + width].astype(F32)
                column += width
        for k in flips:
            outs[k][...] = targets[k][...].T

    return kernel(
        "unpack",
        body,
        [full(mine, FAR), full([got], FAR), full([s], SCALAR)],
        [shaped((w, 2 * h) if k in flips else (2 * h, w), F32) for k, w in enumerate(widths)],
        scratch=[pltpu.VMEM((h, total), BF)] * 2
        + [pltpu.SemaphoreType.DMA((2,))]
        + [pltpu.VMEM((2 * h, widths[k]), F32) for k in flips],
        after=after,
        vmem=20,
    )


def place_out(mine, got, s, after=()):
    shape = mine[0].shape

    def body(ms, gs, ss, outs, scratch):
        side = ss[0][0]
        for layer in range(2):

            @pl.when(side == layer)
            def _():
                copies = [
                    pltpu.make_async_copy(ref, outs[0].at[at], scratch[0].at[k])
                    for k, (ref, at) in enumerate(((ms[layer], layer), (gs[0], 1 - layer)))
                ]
                for copy in copies:
                    copy.start()
                for copy in copies:
                    copy.wait()

    return kernel(
        "place_out",
        body,
        [full(mine, FAR), full([got], FAR), full([s], SCALAR)],
        [shaped((2,) + shape, mine[0].dtype)],
        scratch=[pltpu.SemaphoreType.DMA((2,))],
        after=after,
        vmem=16,
    )[0]


def meet(after):
    def body(outs, _):
        outs[0][...] = jnp.zeros(outs[0].shape, F32)

    return kernel_list("meet", body, [], [shaped((8, 128), F32)], after=after, vmem=2, path=True)


def turn(x, cosine, sine, swap, sign):
    high = x.astype(BF)
    low = (x - high.astype(F32)).astype(BF)
    return x * cosine + (dot(high, swap) + dot(low, swap)) * (sine * sign)


class Fetch:
    def __init__(self, slots, target, sems, column, base=0):
        h, width = slots[0].shape[0], target.shape[1]
        self.target = target
        self.copies = [
            pltpu.make_async_copy(
                ref.at[:, pl.ds(column, width)], target.at[pl.ds(k * h, h), :], sems.at[base + k]
            )
            for k, ref in enumerate(slots)
        ]
        for copy in self.copies:
            copy.start()

    def get(self):
        for copy in self.copies:
            copy.wait()
        return self.target[...]


def pieces_of(value, outs, count, first=0):
    rows = value.shape[0] // count
    for k in range(count):
        outs[first + k][...] = value[k * rows : (k + 1) * rows]


def project(pieces, gain, slots, tables, swaps, width_q, after=()):
    rows, width = pieces[0].shape
    tokens = rows * len(pieces)

    def body(ps, gains, ws, ts, ks, outs, scratch):
        w = Fetch(ws, scratch[0], scratch[1], 0)
        x = stacked(ps).astype(F32)
        scale = lax.rsqrt(jnp.mean(x * x, axis=-1, keepdims=True) + EPSILON)
        n1 = (x * scale * gains[0][...]).astype(BF)
        outs[0][...] = n1
        w.get()
        for part in range(2):
            cols = slice(part * width_q, (part + 1) * width_q)
            raw = dot(n1, scratch[0][:, cols])
            turned = turn(raw, ts[0][:, cols], ts[1][:, cols], ks[part][...], 1.0)
            outs[1 + part][...] = turned.astype(BF)

    return kernel(
        "project",
        body,
        [full(pieces), full([gain]), full(slots, FAR), full(tables), full(swaps)],
        [shaped((tokens, width)), shaped((tokens, width_q)), shaped((tokens, width_q))],
        scratch=[pltpu.VMEM((width, 2 * width_q), BF), pltpu.SemaphoreType.DMA((len(slots),))],
        path=True,
        after=after,
        vmem=24,
        flops=4 * tokens * width * width_q,
    )


def head(ref, at):
    return ref[:, at * HEAD_SIZE : (at + 1) * HEAD_SIZE]


def attention(query, own, there, orders, slots, count, after=()):
    tokens, width_q = query.shape
    rows = tokens // count
    width = slots[0].shape[0] * len(slots)
    heads = width_q // HEAD_SIZE
    kv = heads // 2
    scale = 1.0 / math.sqrt(HEAD_SIZE)

    def body(qs, owns, theres, os, ws, outs, scratch):
        w = Fetch(ws, scratch[0], scratch[1], 2 * width_q)
        seen = os[1][...] <= os[0][...]
        for g in range(kv):
            keys = jnp.concatenate([head(owns[0], g), head(theres[0], g)], 0)
            values = jnp.concatenate([head(owns[0], kv + g), head(theres[0], kv + g)], 0)
            for h in range(2 * g, 2 * g + 2):
                scores = jnp.where(seen, dot_t(keys, head(qs[0], h)), MASKED)
                peak = jnp.max(scores, axis=0, keepdims=True)
                weights = jnp.exp((scores - peak) * scale)
                total = jnp.sum(weights, axis=0, keepdims=True)
                outs[1][h : h + 1, :] = peak * scale + jnp.log(total)
                mixed = t_dot(values, weights.astype(BF)) / total
                outs[0][:, h * HEAD_SIZE : (h + 1) * HEAD_SIZE] = mixed.T.astype(BF)
        pieces_of(dot_t(outs[0][...], w.get()).astype(BF), outs, count, 2)

    mixed, log_sums, *pieces = kernel(
        "attention",
        body,
        [full([query]), full([own]), full([there]), full(orders), full(slots, FAR)],
        [shaped((tokens, width_q)), shaped((heads, tokens), F32)] + [shaped((rows, width))] * count,
        scratch=[pltpu.VMEM((width, width_q), BF), pltpu.SemaphoreType.DMA((len(slots),))],
        path=True,
        after=after,
        vmem=30,
        flops=2 * tokens * width * width_q + 8 * tokens * tokens * width_q,
    )
    return mixed, log_sums, pieces


def attention_back(pieces, query, own, there, log_sums, orders, slots, after=()):
    tokens, width_q = query.shape
    width = slots[0].shape[0] * len(slots)
    heads = width_q // HEAD_SIZE
    kv = heads // 2
    scale = 1.0 / math.sqrt(HEAD_SIZE)

    def body(ps, qs, owns, theres, ls, os, ws, outs, scratch):
        w = Fetch(ws, scratch[0], scratch[1], 2 * width_q)
        seen = os[1][...] <= os[0][...]
        scratch[2][...] = dot(stacked(ps), w.get()).astype(BF)
        for g in range(kv):
            keys = jnp.concatenate([head(owns[0], g), head(theres[0], g)], 0)
            values = jnp.concatenate([head(owns[0], kv + g), head(theres[0], kv + g)], 0)
            sums = [None, None]
            for h in range(2 * g, 2 * g + 2):
                q, grad = head(qs[0], h), head(scratch[2], h)
                scores = dot_t(keys, q) * scale - ls[0][h : h + 1, :]
                probs = jnp.exp(jnp.where(seen, scores, MASKED))
                grad_probs = dot_t(values, grad)
                inner = jnp.sum(probs * grad_probs, axis=0, keepdims=True)
                grad_scores = (probs * (grad_probs - inner)).astype(BF)
                cols = slice(h * HEAD_SIZE, (h + 1) * HEAD_SIZE)
                outs[0][:, cols] = (t_dot(keys, grad_scores) * scale).T
                terms = (dot(grad_scores, q) * scale, dot(probs.astype(BF), grad))
                sums = [t if u is None else t + u for t, u in zip(terms, sums)]
            for at, total in zip((g, kv + g), sums):
                cols = slice(at * HEAD_SIZE, (at + 1) * HEAD_SIZE)
                outs[1][:, cols] = total[:tokens]
                outs[2][:, cols] = total[tokens:].astype(BF)

    return kernel(
        "attention_back",
        body,
        [full(pieces), full([query]), full([own]), full([there]), full([log_sums])]
        + [full(orders), full(slots, FAR)],
        [shaped((tokens, width_q), F32)] * 2 + [shaped((tokens, width_q))],
        scratch=[
            pltpu.VMEM((width, width_q), BF),
            pltpu.SemaphoreType.DMA((len(slots),)),
            pltpu.VMEM((tokens, width_q), BF),
        ],
        path=True,
        after=after,
        vmem=32,
        flops=2 * tokens * width * width_q + 20 * tokens * tokens * width_q,
    )


def project_back(grad_query, grad_own, grad_there, slots, tables, swaps, count, after=()):
    tokens, width_q = grad_query.shape
    rows = tokens // count
    width = slots[0].shape[0] * len(slots)

    def body(qs, owns, theres, ws, ts, ks, outs, scratch):
        w = Fetch(ws, scratch[0], scratch[1], 0)
        grads = (qs[0][...], owns[0][...] + theres[0][...].astype(F32))
        for part in range(2):
            cols = slice(part * width_q, (part + 1) * width_q)
            turned = turn(grads[part], ts[0][:, cols], ts[1][:, cols], ks[part][...], -1.0)
            outs[count][:, cols] = turned.astype(BF)
        pieces_of(dot_t(outs[count][...], w.get()).astype(BF), outs, count)

    *pieces, grads = kernel(
        "project_back",
        body,
        [full([grad_query]), full([grad_own]), full([grad_there]), full(slots, FAR)]
        + [full(tables), full(swaps)],
        [shaped((rows, width))] * count + [shaped((tokens, 2 * width_q))],
        scratch=[pltpu.VMEM((width, 2 * width_q), BF), pltpu.SemaphoreType.DMA((len(slots),))],
        path=True,
        after=after,
        vmem=24,
        flops=4 * tokens * width * width_q,
    )
    return pieces, grads


def feed_forward(pieces, wide, narrow, after=()):
    rows, width = pieces[0].shape
    count = len(pieces)
    tokens = rows * count
    units = wide[0].shape[1] // 3 if wide[0] is narrow[0] else narrow[0].shape[1]
    last = narrow[0].shape[1] - units
    slots = len(wide)

    def body(ps, ws, vs, outs, scratch):
        parts = [
            Fetch(refs, scratch[k], scratch[3], column, k * slots)
            for k, (refs, column) in enumerate(((ws, 0), (ws, units), (vs, last)))
        ]
        n2 = stacked(ps)
        gate = dot(n2, parts[0].get())
        up = dot(n2, parts[1].get())
        outs[0][...] = gate.astype(BF)
        outs[1][...] = up.astype(BF)
        outs[2][...] = (gate / (1.0 + jnp.exp(-gate)) * up).astype(BF)
        pieces_of(dot_t(outs[2][...], parts[2].get()).astype(BF), outs, count, 3)

    gate, up, hidden, *out = kernel(
        "feed_forward",
        body,
        [full(pieces), full(wide, FAR), full(narrow, FAR)],
        [shaped((tokens, units))] * 3 + [shaped((rows, width))] * count,
        scratch=[pltpu.VMEM((width, units), BF)] * 3
        + [pltpu.SemaphoreType.DMA((3 * slots,))],
        path=True,
        after=after,
        vmem=32,
        flops=6 * tokens * width * units,
    )
    return gate, up, hidden, out


def feed_forward_back(pieces, gate, up, wide, narrow, after=()):
    rows, width = pieces[0].shape
    count = len(pieces)
    tokens = rows * count
    units = gate.shape[1]

    last = narrow[0].shape[1] - units
    slots = len(wide)

    def body(ps, gus, ws, vs, outs, scratch):
        down = Fetch(vs, scratch[0], scratch[2], last)
        rest = Fetch(ws, scratch[1], scratch[2], 0, slots)
        grad = dot(stacked(ps), down.get())
        gate, up = gus[0][...].astype(F32), gus[1][...].astype(F32)
        sig = 1.0 / (1.0 + jnp.exp(-gate))
        part = grad * sig
        outs[0][:, :units] = (part * up * (1.0 + gate * (1.0 - sig))).astype(BF)
        outs[0][:, units:] = (part * gate).astype(BF)
        pieces_of(dot_t(outs[0][...], rest.get()).astype(BF), outs, count, 1)

    grads, *out = kernel(
        "feed_forward_back",
        body,
        [full(pieces), full([gate, up]), full(wide, FAR), full(narrow, FAR)],
        [shaped((tokens, 2 * units))] + [shaped((rows, width))] * count,
        scratch=[pltpu.VMEM((width, units), BF), pltpu.VMEM((width, 2 * units), BF)]
        + [pltpu.SemaphoreType.DMA((2 * slots,))],
        path=True,
        after=after,
        vmem=32,
        flops=6 * tokens * width * units,
    )
    return grads, out


def weight_grads(terms, half, block, after=()):
    width = terms[0][0][0].shape[1] // 2
    tokens = terms[0][1].shape[0]
    steps = [rhs.shape[1] // block for _, rhs in terms]
    total = sum(rhs.shape[1] for _, rhs in terms)
    n = 1 if half else lax.axis_size("row")
    rows = width // n
    ins, begins = [], []
    for k, (lhs, rhs) in enumerate(terms):
        begin = sum(steps[:k])
        begins.append(begin)
        ins.append([(a, pl.BlockSpec((a.shape[0], width), lambda j: (0, half))) for a in lhs])
        place = functools.partial(
            lambda j, lo, hi: (0, jnp.clip(j - lo, 0, hi)), lo=begin, hi=steps[k] - 1
        )
        ins.append([(rhs, pl.BlockSpec((tokens, block), place))])

    def body(*refs):
        *refs, outs, scratch = refs
        j = pl.program_id(0)
        for k, begin in enumerate(begins):
            lhs, rhs = refs[2 * k : 2 * k + 2]

            @pl.when(j == begin)
            def _():
                scratch[0][...] = stacked(lhs).T

            @pl.when((j >= begin) & (j < begin + steps[k]))
            def _():
                value = dot(scratch[0][...], rhs[0][...]).astype(BF)
                for k in range(n):
                    outs[k][...] = value[k * rows : (k + 1) * rows]

    return list(
        kernel(
            "weight_grads",
            body,
            ins,
            [shaped((rows, total), BF, pl.BlockSpec((rows, block), lambda j: (0, j)))] * n,
            grid=(sum(steps),),
            scratch=[pltpu.VMEM((width, tokens), BF)],
            after=after,
            vmem=20,
            flops=2 * tokens * width * total,
        )
    )


def add_slots(slot, got, k, come=None, after=()):
    rows, width = slot.shape
    half = width // 2 if width % 256 == 0 else width
    plain = pl.BlockSpec((rows, half), lambda j: (0, j))
    ins = [(slot, plain), (got, pl.BlockSpec((rows, half), lambda j: (k, j)))]
    if come is not None:
        ins.append((come, plain))

    def body(refs, outs, _):
        outs[0][...] = total_of(refs).astype(BF)

    return kernel(
        "add_slots",
        body,
        [ins],
        [shaped(slot.shape, BF, plain)],
        grid=(width // half,),
        after=after,
        vmem=16,
    )[0]


def choose(values, s, after=()):
    def body(vs, ss, outs, scratch):
        for side in range(2):

            @pl.when(ss[0][0] == side)
            def _():
                copy = pltpu.make_async_copy(vs[1 - side], outs[0], scratch[0].at[0])
                copy.start()
                copy.wait()

    return kernel(
        "choose",
        body,
        [full(values, ANYWHERE), full([s], SCALAR)],
        [shaped(values[0].shape, values[0].dtype)],
        scratch=[pltpu.SemaphoreType.DMA((1,))],
        after=after,
        vmem=16,
    )[0]


def sum_gains(terms, s, n):
    h = terms[0].shape[1] // (2 * n)

    def body(ts, ss, outs, _):
        total = total_of(ts)
        for k in range(n):
            first = total[:, k * h : (k + 1) * h]
            second = total[:, (n + k) * h : (n + k + 1) * h]
            for side in range(2):

                @pl.when(ss[0][0] == side)
                def _():
                    low, high = (first, second) if side == 0 else (second, first)
                    outs[k][:, :h] = low
                    outs[k][:, h:] = high

    return kernel(
        "sum_gains",
        body,
        [full(terms), full([s], SCALAR)],
        [shaped((4, 2 * h), F32)] * n,
        vmem=8,
    )


def own_gains(terms, s):
    def body(ts, ss, outs, _):
        total = total_of(ts)
        for side in range(2):

            @pl.when(ss[0][0] == side)
            def _():
                outs[0][...] = total[2 * side : 2 * side + 2]
                outs[1][...] = total[2 - 2 * side : 4 - 2 * side]

    width = terms[0].shape[1]
    return kernel(
        "own_gains",
        body,
        [full(terms), full([s], SCALAR)],
        [shaped((2, width), F32)] * 2,
        vmem=8,
    )


def total_of(refs):
    total = refs[0][...].astype(F32)
    for r in refs[1:]:
        total = total + r[...].astype(F32)
    return total


def inverse_rms(x):
    return lax.rsqrt(jnp.mean(x * x, axis=-1, keepdims=True) + EPSILON)


def add_and_norm(x, terms, gain, after=()):
    def body(xs, ts, gains, outs, _):
        middle = xs[0][...].astype(F32) + total_of(ts)
        outs[0][...] = middle
        outs[1][...] = (middle * inverse_rms(middle) * gains[0][...]).astype(BF)

    return kernel(
        "add_and_norm",
        body,
        [full([x], FETCHED), full(terms, FETCHED), full([gain])],
        [shaped(x.shape, F32), shaped(x.shape)],
        path=True,
        after=after,
        vmem=16,
    )


def add_up(middle, terms, after=()):
    def body(xs, ts, outs, _):
        outs[0][...] = (xs[0][...] + total_of(ts)).astype(BF)

    return kernel(
        "add_up",
        body,
        [full([middle], FETCHED), full(terms, FETCHED)],
        [shaped(middle.shape)],
        after=after,
        vmem=16,
        path=True,
    )[0]


def norm_back(x, terms, gain, straight, after=()):
    def body(xs, ts, gains, ss, outs, _):
        x = xs[0][...].astype(F32)
        grad = total_of(ts)
        scale = inverse_rms(x)
        unit = x * scale
        scaled = grad * gains[0][...]
        outs[0][...] = jnp.sum(grad * unit, axis=0, keepdims=True)
        mean = jnp.mean(scaled * unit, axis=-1, keepdims=True)
        total = ss[0][...].astype(F32) + scale * (scaled - unit * mean)
        outs[1][...] = total
        outs[2][...] = total.astype(BF)

    return kernel(
        "norm_back",
        body,
        [full([x], FETCHED), full(terms, FETCHED), full([gain]), full([straight], FETCHED)],
        [shaped((1, x.shape[1]), F32), shaped(x.shape, F32), shaped(x.shape)],
        path=True,
        after=after,
        vmem=16,
    )


def behind(value, *others):
    return lax.optimization_barrier((value, *others))[0]


def strides(count):
    return [count * (k + 1) // 3 - count * k // 3 for k in range(3)]


class Gather:
    def __init__(self, mine):
        self.slots = [mine]
        self.others = [mate(mine, "section", 1)]
        self.parts = strides(lax.axis_size("row") - 1)

    def hop(self, *now):
        if now:
            self.slots[-1] = behind(self.slots[-1], *now)
        for _ in range(self.parts.pop(0)):
            self.slots.append(ring(self.slots[-1], -1))
            self.others.append(mate(self.slots[-1], "section", 1))
        return [self.slots[-1]]

    def all(self):
        return self.slots + self.others


class Scatter:
    def __init__(self, terms, block):
        other = weight_grads(terms, 1, block)
        self.slots = weight_grads(terms, 0, block)
        self.got = mate(other[0], "section", 1)
        self.made = [self.slots[0], other[0]]
        self.parts = strides(len(self.slots) - 1)
        self.moving = None

    def add(self, come, *now):
        k = len(self.slots) - 1
        self.moving = add_slots(self.slots.pop(), self.got, k, come, now)

    def begin(self, *now):
        if self.moving is None:
            self.add(None, *now)
        else:
            self.moving = behind(self.moving, *now)
        steps = self.parts.pop(0)
        for step in range(steps):
            self.come = ring(self.moving, 1)
            if step < steps - 1:
                self.add(self.come)

    def finish(self, *now):
        self.add(self.come, *now)
        return [self.moving]


def received(pieces):
    return [pieces[0]] + [mate(pieces[k], "col", k) for k in range(1, len(pieces))]


def feature_order(width, s):
    n = lax.axis_size("row")
    i = lax.axis_index("row")
    h = width // (2 * n)
    place = jnp.arange(width)
    part, block, inner = place // (n * h), (place // h) % n, place % h
    source = ((i + block) % n) * 2 * h + ((s + part) % 2) * h + inner
    return (place[:, None] == source[None, :]).astype(BF), (
        source[:, None] == place[None, :]
    ).astype(BF)


def swap_matrix(width, turned):
    source, place = jnp.arange(width)[:, None], jnp.arange(width)[None, :]
    first = (place % HEAD_SIZE) < HALF
    hit = jnp.where(first, source == place + HALF, source == place - HALF) & (place < turned)
    return jnp.where(hit, jnp.where(first, -1.0, 1.0), 0.0).astype(BF)


def token_tables(place, width_q, width_kv):
    power = -(jnp.arange(HALF, dtype=F32) * 2.0) / HEAD_SIZE
    angles = place.astype(F32)[:, None] * (ROPE_BASE**power)[None, :]
    lane = jnp.arange(2 * width_q)
    turned = lane < width_q + width_kv
    spread = (jnp.arange(HALF)[:, None] == (lane % HALF)[None, :]) & turned[None, :]
    rest = jnp.where(turned, 0.0, 1.0).astype(F32)[None, :]
    return spread_tables(jnp.cos(angles), jnp.sin(angles), spread.astype(BF), rest)


def spread_tables(cosine, sine, spread, rest):
    def body(ts, ms, rs, outs, _):
        for k in range(2):
            left, total = ts[k][...], jnp.zeros(outs[k].shape, F32)
            for _ in range(3):
                part = left.astype(BF)
                total = total + dot(part, ms[0][...])
                left = left - part.astype(F32)
            outs[k][...] = total + rs[0][...] if k == 0 else total

    shape = (cosine.shape[0], spread.shape[1])
    return kernel(
        "spread_tables",
        body,
        [full([cosine, sine]), full([spread]), full([rest])],
        [shaped(shape, F32)] * 2,
        vmem=16,
    )


def gather_gains(gains, s):
    terms = [gains] + [mate(gains, "col", k) for k in range(1, lax.axis_size("col"))]
    return list(sum_gains(terms, s, lax.axis_size("row")))


def reduce_gains(slots, s):
    return list(own_gains([slots[0]] + [ring(slots[k], k) for k in range(1, len(slots))], s))


def body(
    inputs,
    positions,
    w_query,
    key_weight,
    value_weight,
    w_out,
    w_gate,
    w_up,
    w_down,
    gain_attn,
    gain_ffn,
    cotangent,
):
    s = lax.axis_index("section")
    c = lax.axis_index("col")
    n = lax.axis_size("row")
    count = lax.axis_size("col")
    width_q, width_kv, units = w_query.shape[2], key_weight.shape[2], w_gate.shape[2]
    tokens, width = inputs.shape[1:]
    rows = tokens // count
    s_here, c_here = s.astype(jnp.int32)[None], c.astype(jnp.int32)[None]

    def start(parts, after):
        keep, send = pack(parts, s_here, after)
        got = mate(send, "section", 1)
        return [jnp.where(s == layer, keep, got) for layer in range(2)]

    flipped = [(jnp.swapaxes(w[0], 0, 1), True) for w in (key_weight, value_weight)]
    attn_start = start((w_query[0], *flipped, w_out[0]), [])
    first = attn_start[0]
    a = Gather(first)
    come = a.hop()
    ffn_start = start((w_gate[0], w_up[0], w_down[0]), [first])
    f = Gather(ffn_start[0])

    gains = behind(jnp.concatenate([gain_attn, gain_ffn], 0), first)
    pair = mate(gains, "section", 1)
    gains = jnp.concatenate([jnp.where(s == 0, gains, pair), jnp.where(s == 0, pair, gains)], 0)
    gains = jnp.stack([gains] + [ring(gains, -k) for k in range(1, n)], 1)
    gains = gains.reshape(4, n, 2, -1)
    gains = jnp.where(s == 0, gains, gains[:, :, ::-1]).transpose(0, 2, 1, 3).reshape(4, 1, -1)
    gains = gains.astype(F32)

    inputs, positions = behind(inputs, first), behind(positions, *come)
    order, back_order = feature_order(width, behind(s, *come))
    swaps = [swap_matrix(width_q, width_q), swap_matrix(width_q, width_kv)]
    x = lax.dynamic_index_in_dim(inputs, s, 0, keepdims=False)
    place = lax.dynamic_index_in_dim(positions, s, 0, keepdims=False)
    cot = lax.dynamic_index_in_dim(cotangent, s, 0, keepdims=False)
    piece = jnp.arange(count) ^ c
    token = (piece[:, None] * rows + jnp.arange(rows)[None, :]).reshape(-1)
    place = jnp.concatenate(
        [lax.dynamic_slice_in_dim(place, (c ^ k) * rows, rows) for k in range(count)]
    )
    tables = token_tables(place, width_q, width_kv)
    parity = lax.axis_index("row") % 2

    def order_of(side):
        half = tokens // 2
        return token + jnp.where(side == 0, jnp.where(token < half, 0, 2 * half), half)

    own_order = order_of(parity)
    orders = [own_order[None, :], jnp.concatenate([own_order, order_of(1 - parity)])[:, None]]

    point = meet(come)
    come = a.hop()
    x = enter(x, order, c_here, count, come + point + f.slots, True)
    a.hop()
    f.hop(*come)
    grad = enter(cot, order, c_here, count)

    kept, outs, gathers = [], [], []
    for layer in range(2):
        gain1, gain2 = gains[2 * layer], gains[2 * layer + 1]
        last = layer == 1
        gathers.append((a, f))
        come = meet(x[1:] + a.slots[-1:] + grad[:1]) if last else []
        n1, query, own = project(x, gain1, a.all(), tables, swaps, width_q, come)
        there = mate(own, "row", 1)
        come = f.hop(there)
        mixed, sums, y = attention(query, own, there, orders, a.all(), count)
        sent = received(y)
        f.hop(sent[-1])
        if not last:
            a, f_old = Gather(attn_start[1]), f
            a.hop(sent[-1])
        middle, n2 = add_and_norm(x[0], sent, gain2, come)
        n2 = gather_pieces(n2)
        point = meet(n2[1:] + f.slots[-1:] + a.slots[-1:])
        if not last:
            f = Gather(ffn_start[1])
            come = f.hop(n2[-1]) + a.hop(n2[-1])
        gate, up, hidden, y = feed_forward(
            n2, gathers[-1][1].all(), gathers[-1][1].all(), point
        )
        kept.append((x[0], n1, query, own, there, mixed, sums, middle, n2, gate, up, hidden))
        if not last:
            sent = received(y)
            a.hop(sent[-1])
            x = gather_pieces(add_up(middle, sent, come))
            outs.append(x)

    def exchange(values):
        return mate(choose(values, s_here), "section", 1)

    left, parts, gain_parts = [None, None], [None, None], [None, None]
    last_y, s_a, come = y, None, []
    for layer in (1, 0):
        a, f = gathers[layer]
        x, n1, query, own, there, mixed, sums, middle, n2, gate, up, hidden = kept[layer]
        gain1, gain2 = gains[2 * layer], gains[2 * layer + 1]
        if s_a:
            s_a.begin(grad[-1])
            s_d.begin(grad[-1])
        grad_gu, y = feed_forward_back(grad, gate, up, f.all(), f.all(), come)
        sent = received(y)
        come = s_a.finish(sent[-1]) + s_d.finish(sent[-1]) if s_a else []
        s_f = Scatter([(n2, grad_gu)], units // 2)
        come += s_f.made
        s_f.begin(sent[-1])
        if s_a:
            s_a.begin(sent[-1])
        g_gain2, grad_middle, grad_attn = norm_back(middle, sent, gain2, grad[0], come)
        s_d = Scatter([(grad, behind(hidden, grad_attn))], units // 2)
        grad_attn = gather_pieces(grad_attn)
        come = s_d.made + s_f.finish(grad_attn[-1]) + (s_a.finish(grad_attn[-1]) if s_a else [])
        s_d.begin(grad_attn[-1])
        grad_query, grad_own, grad_there = attention_back(
            grad_attn, query, own, there, sums, orders, a.all(), come
        )
        if layer == 1:
            last_y = received([behind(p, grad_attn[-1]) for p in last_y])
            left[0] = leave([behind(p, grad_there) for p in outs[0]], back_order, c_here)
            come = last_y[1:] + [left[0]]
        else:
            outs.append(gather_pieces(add_up(kept[1][7], last_y, grad_attn[-1:])))
            left[1] = leave([behind(p, grad_there) for p in grad], back_order, c_here)
            come = outs[1][1:] + [left[1]]
        back = mate(grad_there, "row", 1)
        come += s_d.finish(back)
        s_f.begin(back)
        s_d.begin(back)
        y, grad_qkv = project_back(
            grad_query, grad_own, back, a.all(), tables, swaps, count, come
        )
        sent = received(y)
        come = s_f.finish(sent[-1]) + s_d.finish(sent[-1])
        s_a = Scatter([([n1], grad_qkv), (grad_attn, mixed)], width_q)
        s_f.begin(sent[-1])
        s_a.begin(sent[-1])
        g_gain1, _, grad = norm_back(x, sent, gain1, grad_middle, come + s_a.made)
        mark = meet([grad])
        grad = gather_pieces(grad)
        come = s_f.finish(grad[-1]) + s_a.finish(grad[-1])
        parts[layer] = (s_a, s_f, s_d)
        gain_parts[layer] = (g_gain1, g_gain2)

    acts = [left[0], leave([behind(p, *mark) for p in outs[1]], back_order, c_here)]
    point = meet(grad[1:] + acts[1:] + come + mark)
    s_a.begin(*point)
    s_d.begin(*point)
    mark = meet(point)
    grads = [leave([behind(p, *mark) for p in grad], back_order, c_here, path=True), left[1]]
    grads_got = exchange(grads)
    acts_got = exchange([behind(v, *mark) for v in acts])
    wide = [p[1].moving for p in parts]
    wide_got = exchange([behind(v, *mark) for v in wide])
    gain_grads = jnp.concatenate(list(gain_parts[0]) + list(gain_parts[1]), 0)
    gain_slots = gather_gains(behind(gain_grads, grads[0]), s_here)
    point = meet(s_a.finish(grads[0]) + s_d.finish(grads[0]) + gain_slots + mark)
    s_a.begin(*point)
    mark = meet(point)
    acts = place_out([behind(v, *mark) for v in acts], acts_got, s_here)
    grads = place_out([behind(v, *mark) for v in grads], grads_got, s_here)
    g_gate, g_up = unpack([behind(v, *mark) for v in wide], wide_got, s_here, (units, units))
    gain_grads = reduce_gains(gain_slots, s_here)
    s_a.finish(grads, acts, g_up, *gain_grads)
    gain_grads = gain_grads[0] + mate(gain_grads[1], "section", 1)
    heads, narrow = ([p[k].moving for p in parts] for k in (0, 2))
    heads_got, narrow_got = exchange(heads), exchange(narrow)
    point = meet([heads_got, narrow_got, g_up, acts, grads])
    (g_down,) = unpack(narrow, narrow_got, s_here, (units,), point)
    g_query, g_key, g_value, g_out = unpack(
        heads, heads_got, s_here, (width_q, width_kv, width_kv, width_q), point, (1, 2)
    )
    g_key, g_value = jnp.swapaxes(g_key, 0, 1), jnp.swapaxes(g_value, 0, 1)
    return (
        acts[None],
        grads[None],
        *[g[None] for g in (g_query, g_key, g_value, g_out, g_gate, g_up, g_down)],
        gain_grads[0:1],
        gain_grads[1:2],
    )


def solution(mesh):
    placed = (
        P(None, "row", None),
        P(None, "row"),
        *[P("section", "row", "col")] * 7,
        *[P("section", "row")] * 2,
        P(None, "row", None),
    )
    return jax.shard_map(
        body,
        mesh=mesh,
        in_specs=placed,
        out_specs=(
            *[P("section", None, "row", None)] * 2,
            *[P("section", "row", "col")] * 7,
            *[P("section", "row")] * 2,
        ),
        check_vma=False,
    )
```

```python
import functools
import math

import jax
import jax.numpy as jnp
from jax import lax
from jax.experimental import pallas as pl
from jax.experimental.pallas import tpu as pltpu
from jax.sharding import PartitionSpec as P

HEAD_SIZE = 96
HALF = HEAD_SIZE // 2
EPSILON = 1e-05
ROPE_BASE = 100000.0
MASKED = -1e30
COST = 60000000000
COSTS = {'add_slots': 3000000000, 'choose': 2000000000, 'sum_gains': 1000000000, 'own_gains': 1000000000}
BF = jnp.bfloat16
F32 = jnp.float32
WHOLE = pl.BlockSpec(memory_space=pltpu.VMEM)
ANYWHERE = pl.BlockSpec(memory_space=pl.ANY)
FAR = pl.BlockSpec(memory_space=pltpu.HBM)
FETCHED = object()
NEAR = object()
SCALAR = pl.BlockSpec(memory_space=pltpu.SMEM)


def mate(x, axis, k):
    n = lax.axis_size(axis)
    return lax.ppermute(x, axis, [(j, j ^ k) for j in range(n)])


def ring(x, by):
    n = lax.axis_size("row")
    return lax.ppermute(x, "row", [(j, (j + by) % n) for j in range(n)])


def gather_pieces(local):
    return [local] + [mate(local, "col", k) for k in range(1, lax.axis_size("col"))]


def dot(left, right):
    return jnp.dot(left, right, preferred_element_type=F32)


def dot_t(left, right):
    return lax.dot_general(left, right, (((1,), (1,)), ((), ())), preferred_element_type=F32)


def t_dot(left, right):
    return lax.dot_general(left, right, (((0,), (0,)), ((), ())), preferred_element_type=F32)


def stacked(refs):
    return jnp.concatenate([r[...] for r in refs], axis=0)


def kernel(name, body, ins, outs, grid=(), scratch=(), after=(), vmem=44, flops=0, path=False):
    arrays, specs, sizes, fetched = [], [], [], []
    for group in ins:
        sizes.append(len(group))
        for array, spec in group:
            if spec is FETCHED or spec is NEAR:
                fetched.append(len(arrays))
            arrays.append(array)
            specs.append(FAR if spec is FETCHED else ANYWHERE if spec is NEAR else spec)
    count = len(arrays)
    after = list(after)
    arrays += after
    specs += [ANYWHERE] * len(after)
    targets = [pltpu.VMEM(arrays[k].shape, arrays[k].dtype) for k in fetched]
    if fetched:
        targets.append(pltpu.SemaphoreType.DMA((len(fetched),)))

    def run(*refs):
        refs = list(refs)
        extra = refs[len(refs) - len(targets) :] if targets else []
        refs = refs[: len(refs) - len(targets)]
        copies = [
            pltpu.make_async_copy(refs[k], extra[j], extra[-1].at[j])
            for j, k in enumerate(fetched)
        ]
        for copy in copies:
            copy.start()
        for copy in copies:
            copy.wait()
        for j, k in enumerate(fetched):
            refs[k] = extra[j]
        groups, at = [], 0
        for size in sizes:
            groups.append(refs[at : at + size])
            at += size
        at = count + len(after)
        body(*groups, refs[at : at + len(outs)], refs[at + len(outs) :])

    size = sum(a.size * a.dtype.itemsize for a in arrays[:count])
    size += sum(math.prod(o.shape) * jnp.dtype(o.dtype).itemsize for o, _ in outs)
    return pl.pallas_call(
        run,
        grid=grid,
        in_specs=specs,
        out_specs=[spec for _, spec in outs],
        out_shape=[shape for shape, _ in outs],
        scratch_shapes=list(scratch) + targets,
        compiler_params=pltpu.CompilerParams(vmem_limit_bytes=vmem << 20),
        cost_estimate=pl.CostEstimate(
            flops=COST if path else COSTS.get(name, 0),
            bytes_accessed=size if path else 1,
            transcendentals=0,
        ),
        name=name,
    )(*arrays)


def kernel_list(*args, **settings):
    return list(kernel(*args, **settings))


def shaped(shape, dtype=BF, spec=WHOLE):
    return (jax.ShapeDtypeStruct(tuple(shape), dtype), spec)


def full(arrays, spec=WHOLE):
    return [(a, spec) for a in arrays]


def enter(x, order, c, count, after=(), path=False):
    rows = x.shape[0] // count

    def body(xs, orders, cs, outs, _):
        for k in range(count):
            start = pl.multiple_of((cs[0][0] ^ k) * rows, 16)
            outs[k][...] = dot(xs[0][pl.ds(start, rows), :], orders[0][...]).astype(BF)

    return kernel_list(
        "enter",
        body,
        [full([x], FETCHED), full([order], FETCHED), full([c], SCALAR)],
        [shaped((rows, x.shape[1]))] * count,
        after=after,
        vmem=16,
        path=path,
    )


def leave(pieces, back, c, after=(), path=False):
    rows, width = pieces[0].shape
    count = len(pieces)

    def body(ps, orders, cs, outs, _):
        y = dot(stacked(ps), orders[0][...]).astype(BF)
        for k in range(count):
            start = pl.multiple_of((cs[0][0] ^ k) * rows, 16)
            outs[0][pl.ds(start, rows), :] = y[k * rows : (k + 1) * rows]

    return kernel(
        "leave",
        body,
        [full(pieces), full([back]), full([c], SCALAR)],
        [shaped((rows * count, width))],
        after=after,
        vmem=20,
        path=path,
        flops=2 * rows * count * width * width,
    )[0]


def pack(parts, s, after=()):
    flips = [isinstance(p, tuple) for p in parts]
    parts = [p[0] if flip else p for p, flip in zip(parts, flips)]
    shapes = [p.shape[::-1] if flip else p.shape for p, flip in zip(parts, flips)]
    h = shapes[0][0] // 2
    width = sum(shape[1] for shape in shapes)

    def body(ps, ss, outs, scratch):
        scratch, sources = list(scratch), []
        for p, flip in zip(ps, flips):
            if flip:
                sources.append(scratch.pop(0))
                sources[-1][...] = p[...].T
            else:
                sources.append(p)
        for out, side in zip(outs, (ss[0][0], 1 - ss[0][0])):
            start = pl.multiple_of(side * h, 16)
            at = 0
            for p in sources:
                out[:, at : at + p.shape[1]] = p[pl.ds(start, h), :]
                at += p.shape[1]

    return kernel(
        "pack",
        body,
        [full(parts, FETCHED), full([s], SCALAR)],
        [shaped((h, width))] * 2,
        scratch=[pltpu.VMEM(shape, BF) for shape, flip in zip(shapes, flips) if flip],
        after=after,
        vmem=16,
    )


def unpack(mine, got, s, widths, after=(), flips=()):
    h, total = mine[0].shape

    def body(ms, gs, ss, outs, scratch):
        side = ss[0][0]
        for layer in range(2):

            @pl.when(side == layer)
            def _():
                copies = [
                    pltpu.make_async_copy(ref, scratch[k], scratch[2].at[k])
                    for k, ref in enumerate((ms[layer], gs[0]))
                ]
                for copy in copies:
                    copy.start()
                for copy in copies:
                    copy.wait()

        turned = list(scratch[3:])
        targets = [turned.pop(0) if k in flips else out for k, out in enumerate(outs)]
        for k, at in enumerate((side, 1 - side)):
            start = pl.multiple_of(at * h, 16)
            column = 0
            for target in targets:
                width = target.shape[1]
                target[pl.ds(start, h), :] = scratch[k][:, column : column + width].astype(F32)
                column += width
        for k in flips:
            outs[k][...] = targets[k][...].T

    return kernel(
        "unpack",
        body,
        [full(mine, FAR), full([got], FAR), full([s], SCALAR)],
        [shaped((w, 2 * h) if k in flips else (2 * h, w), F32) for k, w in enumerate(widths)],
        scratch=[pltpu.VMEM((h, total), BF)] * 2
        + [pltpu.SemaphoreType.DMA((2,))]
        + [pltpu.VMEM((2 * h, widths[k]), F32) for k in flips],
        after=after,
        vmem=20,
    )


def place_out(mine, got, s, after=()):
    shape = mine[0].shape

    def body(ms, gs, ss, outs, scratch):
        side = ss[0][0]
        for layer in range(2):

            @pl.when(side == layer)
            def _():
                copies = [
                    pltpu.make_async_copy(ref, outs[0].at[at], scratch[0].at[k])
                    for k, (ref, at) in enumerate(((ms[layer], layer), (gs[0], 1 - layer)))
                ]
                for copy in copies:
                    copy.start()
                for copy in copies:
                    copy.wait()

    return kernel(
        "place_out",
        body,
        [full(mine, FAR), full([got], FAR), full([s], SCALAR)],
        [shaped((2,) + shape, mine[0].dtype)],
        scratch=[pltpu.SemaphoreType.DMA((2,))],
        after=after,
        vmem=16,
    )[0]


def meet(after):
    def body(outs, _):
        outs[0][...] = jnp.zeros(outs[0].shape, F32)

    return kernel_list("meet", body, [], [shaped((8, 128), F32)], after=after, vmem=2, path=True)


def turn(x, cosine, sine, swap, sign):
    high = x.astype(BF)
    low = (x - high.astype(F32)).astype(BF)
    return x * cosine + (dot(high, swap) + dot(low, swap)) * (sine * sign)


class Fetch:
    def __init__(self, slots, target, sems, column, base=0):
        h, width = slots[0].shape[0], target.shape[1]
        self.target = target
        self.copies = [
            pltpu.make_async_copy(
                ref.at[:, pl.ds(column, width)], target.at[pl.ds(k * h, h), :], sems.at[base + k]
            )
            for k, ref in enumerate(slots)
        ]
        for copy in self.copies:
            copy.start()

    def get(self):
        for copy in self.copies:
            copy.wait()
        return self.target[...]


def pieces_of(value, outs, count, first=0):
    rows = value.shape[0] // count
    for k in range(count):
        outs[first + k][...] = value[k * rows : (k + 1) * rows]


def project(pieces, gain, slots, tables, swaps, width_q, after=()):
    rows, width = pieces[0].shape
    tokens = rows * len(pieces)

    def body(ps, gains, ws, ts, ks, outs, scratch):
        w = Fetch(ws, scratch[0], scratch[1], 0)
        x = stacked(ps).astype(F32)
        scale = lax.rsqrt(jnp.mean(x * x, axis=-1, keepdims=True) + EPSILON)
        n1 = (x * scale * gains[0][...]).astype(BF)
        outs[0][...] = n1
        w.get()
        for part in range(2):
            cols = slice(part * width_q, (part + 1) * width_q)
            raw = dot(n1, scratch[0][:, cols])
            turned = turn(raw, ts[0][:, cols], ts[1][:, cols], ks[part][...], 1.0)
            outs[1 + part][...] = turned.astype(BF)

    return kernel(
        "project",
        body,
        [full(pieces), full([gain]), full(slots, FAR), full(tables), full(swaps)],
        [shaped((tokens, width)), shaped((tokens, width_q)), shaped((tokens, width_q))],
        scratch=[pltpu.VMEM((width, 2 * width_q), BF), pltpu.SemaphoreType.DMA((len(slots),))],
        path=True,
        after=after,
        vmem=24,
        flops=4 * tokens * width * width_q,
    )


def head(ref, at):
    return ref[:, at * HEAD_SIZE : (at + 1) * HEAD_SIZE]


def attention(query, own, there, orders, slots, count, after=()):
    tokens, width_q = query.shape
    rows = tokens // count
    width = slots[0].shape[0] * len(slots)
    heads = width_q // HEAD_SIZE
    kv = heads // 2
    scale = 1.0 / math.sqrt(HEAD_SIZE)

    def body(qs, owns, theres, os, ws, outs, scratch):
        w = Fetch(ws, scratch[0], scratch[1], 2 * width_q)
        seen = os[1][...] <= os[0][...]
        for g in range(kv):
            keys = jnp.concatenate([head(owns[0], g), head(theres[0], g)], 0)
            values = jnp.concatenate([head(owns[0], kv + g), head(theres[0], kv + g)], 0)
            for h in range(2 * g, 2 * g + 2):
                scores = jnp.where(seen, dot_t(keys, head(qs[0], h)), MASKED)
                peak = jnp.max(scores, axis=0, keepdims=True)
                weights = jnp.exp((scores - peak) * scale)
                total = jnp.sum(weights, axis=0, keepdims=True)
                outs[1][h : h + 1, :] = peak * scale + jnp.log(total)
                mixed = t_dot(values, weights.astype(BF)) / total
                outs[0][:, h * HEAD_SIZE : (h + 1) * HEAD_SIZE] = mixed.T.astype(BF)
        pieces_of(dot_t(outs[0][...], w.get()).astype(BF), outs, count, 2)

    mixed, log_sums, *pieces = kernel(
        "attention",
        body,
        [full([query]), full([own]), full([there]), full(orders), full(slots, FAR)],
        [shaped((tokens, width_q)), shaped((heads, tokens), F32)] + [shaped((rows, width))] * count,
        scratch=[pltpu.VMEM((width, width_q), BF), pltpu.SemaphoreType.DMA((len(slots),))],
        path=True,
        after=after,
        vmem=30,
        flops=2 * tokens * width * width_q + 8 * tokens * tokens * width_q,
    )
    return mixed, log_sums, pieces


def attention_back(pieces, query, own, there, log_sums, orders, slots, after=()):
    tokens, width_q = query.shape
    width = slots[0].shape[0] * len(slots)
    heads = width_q // HEAD_SIZE
    kv = heads // 2
    scale = 1.0 / math.sqrt(HEAD_SIZE)

    def body(ps, qs, owns, theres, ls, os, ws, outs, scratch):
        w = Fetch(ws, scratch[0], scratch[1], 2 * width_q)
        seen = os[1][...] <= os[0][...]
        scratch[2][...] = dot(stacked(ps), w.get()).astype(BF)
        for g in range(kv):
            keys = jnp.concatenate([head(owns[0], g), head(theres[0], g)], 0)
            values = jnp.concatenate([head(owns[0], kv + g), head(theres[0], kv + g)], 0)
            sums = [None, None]
            for h in range(2 * g, 2 * g + 2):
                q, grad = head(qs[0], h), head(scratch[2], h)
                scores = dot_t(keys, q) * scale - ls[0][h : h + 1, :]
                probs = jnp.exp(jnp.where(seen, scores, MASKED))
                grad_probs = dot_t(values, grad)
                inner = jnp.sum(probs * grad_probs, axis=0, keepdims=True)
                grad_scores = (probs * (grad_probs - inner)).astype(BF)
                cols = slice(h * HEAD_SIZE, (h + 1) * HEAD_SIZE)
                outs[0][:, cols] = (t_dot(keys, grad_scores) * scale).T
                terms = (dot(grad_scores, q) * scale, dot(probs.astype(BF), grad))
                sums = [t if u is None else t + u for t, u in zip(terms, sums)]
            for at, total in zip((g, kv + g), sums):
                cols = slice(at * HEAD_SIZE, (at + 1) * HEAD_SIZE)
                outs[1][:, cols] = total[:tokens]
                outs[2][:, cols] = total[tokens:].astype(BF)

    return kernel(
        "attention_back",
        body,
        [full(pieces), full([query]), full([own]), full([there]), full([log_sums])]
        + [full(orders), full(slots, FAR)],
        [shaped((tokens, width_q), F32)] * 2 + [shaped((tokens, width_q))],
        scratch=[
            pltpu.VMEM((width, width_q), BF),
            pltpu.SemaphoreType.DMA((len(slots),)),
            pltpu.VMEM((tokens, width_q), BF),
        ],
        path=True,
        after=after,
        vmem=32,
        flops=2 * tokens * width * width_q + 20 * tokens * tokens * width_q,
    )


def project_back(grad_query, grad_own, grad_there, slots, tables, swaps, count, after=()):
    tokens, width_q = grad_query.shape
    rows = tokens // count
    width = slots[0].shape[0] * len(slots)

    def body(qs, owns, theres, ws, ts, ks, outs, scratch):
        w = Fetch(ws, scratch[0], scratch[1], 0)
        grads = (qs[0][...], owns[0][...] + theres[0][...].astype(F32))
        for part in range(2):
            cols = slice(part * width_q, (part + 1) * width_q)
            turned = turn(grads[part], ts[0][:, cols], ts[1][:, cols], ks[part][...], -1.0)
            outs[count][:, cols] = turned.astype(BF)
        pieces_of(dot_t(outs[count][...], w.get()).astype(BF), outs, count)

    *pieces, grads = kernel(
        "project_back",
        body,
        [full([grad_query]), full([grad_own]), full([grad_there]), full(slots, FAR)]
        + [full(tables), full(swaps)],
        [shaped((rows, width))] * count + [shaped((tokens, 2 * width_q))],
        scratch=[pltpu.VMEM((width, 2 * width_q), BF), pltpu.SemaphoreType.DMA((len(slots),))],
        path=True,
        after=after,
        vmem=24,
        flops=4 * tokens * width * width_q,
    )
    return pieces, grads


def feed_forward(pieces, wide, narrow, after=()):
    rows, width = pieces[0].shape
    count = len(pieces)
    tokens = rows * count
    units = wide[0].shape[1] // 3 if wide[0] is narrow[0] else narrow[0].shape[1]
    last = narrow[0].shape[1] - units
    slots = len(wide)

    def body(ps, ws, vs, outs, scratch):
        parts = [
            Fetch(refs, scratch[k], scratch[3], column, k * slots)
            for k, (refs, column) in enumerate(((ws, 0), (ws, units), (vs, last)))
        ]
        n2 = stacked(ps)
        gate = dot(n2, parts[0].get())
        up = dot(n2, parts[1].get())
        outs[0][...] = gate.astype(BF)
        outs[1][...] = up.astype(BF)
        outs[2][...] = (gate / (1.0 + jnp.exp(-gate)) * up).astype(BF)
        pieces_of(dot_t(outs[2][...], parts[2].get()).astype(BF), outs, count, 3)

    gate, up, hidden, *out = kernel(
        "feed_forward",
        body,
        [full(pieces), full(wide, FAR), full(narrow, FAR)],
        [shaped((tokens, units))] * 3 + [shaped((rows, width))] * count,
        scratch=[pltpu.VMEM((width, units), BF)] * 3
        + [pltpu.SemaphoreType.DMA((3 * slots,))],
        path=True,
        after=after,
        vmem=32,
        flops=6 * tokens * width * units,
    )
    return gate, up, hidden, out


def feed_forward_back(pieces, gate, up, wide, narrow, after=()):
    rows, width = pieces[0].shape
    count = len(pieces)
    tokens = rows * count
    units = gate.shape[1]

    last = narrow[0].shape[1] - units
    slots = len(wide)

    def body(ps, gus, ws, vs, outs, scratch):
        down = Fetch(vs, scratch[0], scratch[2], last)
        rest = Fetch(ws, scratch[1], scratch[2], 0, slots)
        grad = dot(stacked(ps), down.get())
        gate, up = gus[0][...].astype(F32), gus[1][...].astype(F32)
        sig = 1.0 / (1.0 + jnp.exp(-gate))
        part = grad * sig
        outs[0][:, :units] = (part * up * (1.0 + gate * (1.0 - sig))).astype(BF)
        outs[0][:, units:] = (part * gate).astype(BF)
        pieces_of(dot_t(outs[0][...], rest.get()).astype(BF), outs, count, 1)

    grads, *out = kernel(
        "feed_forward_back",
        body,
        [full(pieces), full([gate, up]), full(wide, FAR), full(narrow, FAR)],
        [shaped((tokens, 2 * units))] + [shaped((rows, width))] * count,
        scratch=[pltpu.VMEM((width, units), BF), pltpu.VMEM((width, 2 * units), BF)]
        + [pltpu.SemaphoreType.DMA((2 * slots,))],
        path=True,
        after=after,
        vmem=32,
        flops=6 * tokens * width * units,
    )
    return grads, out


def weight_grads(terms, half, block, after=()):
    width = terms[0][0][0].shape[1] // 2
    tokens = terms[0][1].shape[0]
    steps = [rhs.shape[1] // block for _, rhs in terms]
    total = sum(rhs.shape[1] for _, rhs in terms)
    n = 1 if half else lax.axis_size("row")
    rows = width // n
    ins, begins = [], []
    for k, (lhs, rhs) in enumerate(terms):
        begin = sum(steps[:k])
        begins.append(begin)
        ins.append([(a, pl.BlockSpec((a.shape[0], width), lambda j: (0, half))) for a in lhs])
        place = functools.partial(
            lambda j, lo, hi: (0, jnp.clip(j - lo, 0, hi)), lo=begin, hi=steps[k] - 1
        )
        ins.append([(rhs, pl.BlockSpec((tokens, block), place))])

    def body(*refs):
        *refs, outs, scratch = refs
        j = pl.program_id(0)
        for k, begin in enumerate(begins):
            lhs, rhs = refs[2 * k : 2 * k + 2]

            @pl.when(j == begin)
            def _():
                scratch[0][...] = stacked(lhs).T

            @pl.when((j >= begin) & (j < begin + steps[k]))
            def _():
                value = dot(scratch[0][...], rhs[0][...]).astype(BF)
                for k in range(n):
                    outs[k][...] = value[k * rows : (k + 1) * rows]

    return list(
        kernel(
            "weight_grads",
            body,
            ins,
            [shaped((rows, total), BF, pl.BlockSpec((rows, block), lambda j: (0, j)))] * n,
            grid=(sum(steps),),
            scratch=[pltpu.VMEM((width, tokens), BF)],
            after=after,
            vmem=20,
            flops=2 * tokens * width * total,
        )
    )


def add_slots(slot, got, k, come=None, after=()):
    rows, width = slot.shape
    half = width // 2 if width % 256 == 0 else width
    plain = pl.BlockSpec((rows, half), lambda j: (0, j))
    ins = [(slot, plain), (got, pl.BlockSpec((rows, half), lambda j: (k, j)))]
    if come is not None:
        ins.append((come, plain))

    def body(refs, outs, _):
        outs[0][...] = total_of(refs).astype(BF)

    return kernel(
        "add_slots",
        body,
        [ins],
        [shaped(slot.shape, BF, plain)],
        grid=(width // half,),
        after=after,
        vmem=16,
    )[0]


def choose(values, s, after=()):
    def body(vs, ss, outs, scratch):
        for side in range(2):

            @pl.when(ss[0][0] == side)
            def _():
                copy = pltpu.make_async_copy(vs[1 - side], outs[0], scratch[0].at[0])
                copy.start()
                copy.wait()

    return kernel(
        "choose",
        body,
        [full(values, ANYWHERE), full([s], SCALAR)],
        [shaped(values[0].shape, values[0].dtype)],
        scratch=[pltpu.SemaphoreType.DMA((1,))],
        after=after,
        vmem=16,
    )[0]


def sum_gains(terms, s, n):
    h = terms[0].shape[1] // (2 * n)

    def body(ts, ss, outs, _):
        total = total_of(ts)
        for k in range(n):
            first = total[:, k * h : (k + 1) * h]
            second = total[:, (n + k) * h : (n + k + 1) * h]
            for side in range(2):

                @pl.when(ss[0][0] == side)
                def _():
                    low, high = (first, second) if side == 0 else (second, first)
                    outs[k][:, :h] = low
                    outs[k][:, h:] = high

    return kernel(
        "sum_gains",
        body,
        [full(terms), full([s], SCALAR)],
        [shaped((4, 2 * h), F32)] * n,
        vmem=8,
    )


def own_gains(terms, s):
    def body(ts, ss, outs, _):
        total = total_of(ts)
        for side in range(2):

            @pl.when(ss[0][0] == side)
            def _():
                outs[0][...] = total[2 * side : 2 * side + 2]
                outs[1][...] = total[2 - 2 * side : 4 - 2 * side]

    width = terms[0].shape[1]
    return kernel(
        "own_gains",
        body,
        [full(terms), full([s], SCALAR)],
        [shaped((2, width), F32)] * 2,
        vmem=8,
    )


def total_of(refs):
    total = refs[0][...].astype(F32)
    for r in refs[1:]:
        total = total + r[...].astype(F32)
    return total


def inverse_rms(x):
    return lax.rsqrt(jnp.mean(x * x, axis=-1, keepdims=True) + EPSILON)


def add_and_norm(x, terms, gain, after=()):
    def body(xs, ts, gains, outs, _):
        middle = xs[0][...].astype(F32) + total_of(ts)
        outs[0][...] = middle
        outs[1][...] = (middle * inverse_rms(middle) * gains[0][...]).astype(BF)

    return kernel(
        "add_and_norm",
        body,
        [full([x], FETCHED), full(terms, FETCHED), full([gain])],
        [shaped(x.shape, F32), shaped(x.shape)],
        path=True,
        after=after,
        vmem=16,
    )


def add_up(middle, terms, after=()):
    def body(xs, ts, outs, _):
        outs[0][...] = (xs[0][...] + total_of(ts)).astype(BF)

    return kernel(
        "add_up",
        body,
        [full([middle], FETCHED), full(terms, FETCHED)],
        [shaped(middle.shape)],
        after=after,
        vmem=16,
        path=True,
    )[0]


def norm_back(x, terms, gain, straight, after=()):
    def body(xs, ts, gains, ss, outs, _):
        x = xs[0][...].astype(F32)
        grad = total_of(ts)
        scale = inverse_rms(x)
        unit = x * scale
        scaled = grad * gains[0][...]
        outs[0][...] = jnp.sum(grad * unit, axis=0, keepdims=True)
        mean = jnp.mean(scaled * unit, axis=-1, keepdims=True)
        total = ss[0][...].astype(F32) + scale * (scaled - unit * mean)
        outs[1][...] = total
        outs[2][...] = total.astype(BF)

    return kernel(
        "norm_back",
        body,
        [full([x], FETCHED), full(terms, FETCHED), full([gain]), full([straight], FETCHED)],
        [shaped((1, x.shape[1]), F32), shaped(x.shape, F32), shaped(x.shape)],
        path=True,
        after=after,
        vmem=16,
    )


def behind(value, *others):
    return lax.optimization_barrier((value, *others))[0]


def strides(count):
    return [count * (k + 1) // 3 - count * k // 3 for k in range(3)]


class Gather:
    def __init__(self, mine):
        self.slots = [mine]
        self.others = [mate(mine, "section", 1)]
        self.parts = strides(lax.axis_size("row") - 1)

    def hop(self, *now):
        if now:
            self.slots[-1] = behind(self.slots[-1], *now)
        for _ in range(self.parts.pop(0)):
            self.slots.append(ring(self.slots[-1], -1))
            self.others.append(mate(self.slots[-1], "section", 1))
        return [self.slots[-1]]

    def all(self):
        return self.slots + self.others


class Scatter:
    def __init__(self, terms, block):
        other = weight_grads(terms, 1, block)
        self.slots = weight_grads(terms, 0, block)
        self.got = mate(other[0], "section", 1)
        self.made = [self.slots[0], other[0]]
        self.parts = strides(len(self.slots) - 1)
        self.moving = None

    def add(self, come, *now):
        k = len(self.slots) - 1
        self.moving = add_slots(self.slots.pop(), self.got, k, come, now)

    def begin(self, *now):
        if self.moving is None:
            self.add(None, *now)
        else:
            self.moving = behind(self.moving, *now)
        steps = self.parts.pop(0)
        for step in range(steps):
            self.come = ring(self.moving, 1)
            if step < steps - 1:
                self.add(self.come)

    def finish(self, *now):
        self.add(self.come, *now)
        return [self.moving]


def received(pieces):
    return [pieces[0]] + [mate(pieces[k], "col", k) for k in range(1, len(pieces))]


def feature_order(width, s):
    n = lax.axis_size("row")
    i = lax.axis_index("row")
    h = width // (2 * n)
    place = jnp.arange(width)
    part, block, inner = place // (n * h), (place // h) % n, place % h
    source = ((i + block) % n) * 2 * h + ((s + part) % 2) * h + inner
    return (place[:, None] == source[None, :]).astype(BF), (
        source[:, None] == place[None, :]
    ).astype(BF)


def swap_matrix(width, turned):
    source, place = jnp.arange(width)[:, None], jnp.arange(width)[None, :]
    first = (place % HEAD_SIZE) < HALF
    hit = jnp.where(first, source == place + HALF, source == place - HALF) & (place < turned)
    return jnp.where(hit, jnp.where(first, -1.0, 1.0), 0.0).astype(BF)


def token_tables(place, width_q, width_kv):
    power = -(jnp.arange(HALF, dtype=F32) * 2.0) / HEAD_SIZE
    angles = place.astype(F32)[:, None] * (ROPE_BASE**power)[None, :]
    lane = jnp.arange(2 * width_q)
    turned = lane < width_q + width_kv
    spread = (jnp.arange(HALF)[:, None] == (lane % HALF)[None, :]) & turned[None, :]
    rest = jnp.where(turned, 0.0, 1.0).astype(F32)[None, :]
    return spread_tables(jnp.cos(angles), jnp.sin(angles), spread.astype(BF), rest)


def spread_tables(cosine, sine, spread, rest):
    def body(ts, ms, rs, outs, _):
        for k in range(2):
            left, total = ts[k][...], jnp.zeros(outs[k].shape, F32)
            for _ in range(3):
                part = left.astype(BF)
                total = total + dot(part, ms[0][...])
                left = left - part.astype(F32)
            outs[k][...] = total + rs[0][...] if k == 0 else total

    shape = (cosine.shape[0], spread.shape[1])
    return kernel(
        "spread_tables",
        body,
        [full([cosine, sine]), full([spread]), full([rest])],
        [shaped(shape, F32)] * 2,
        vmem=16,
    )


def gather_gains(gains, s):
    terms = [gains] + [mate(gains, "col", k) for k in range(1, lax.axis_size("col"))]
    return list(sum_gains(terms, s, lax.axis_size("row")))


def reduce_gains(slots, s):
    return list(own_gains([slots[0]] + [ring(slots[k], k) for k in range(1, len(slots))], s))


def body(
    inputs,
    positions,
    w_query,
    key_weight,
    value_weight,
    w_out,
    w_gate,
    w_up,
    w_down,
    gain_attn,
    gain_ffn,
    cotangent,
):
    s = lax.axis_index("section")
    c = lax.axis_index("col")
    n = lax.axis_size("row")
    count = lax.axis_size("col")
    width_q, width_kv, units = w_query.shape[2], key_weight.shape[2], w_gate.shape[2]
    tokens, width = inputs.shape[1:]
    rows = tokens // count
    s_here, c_here = s.astype(jnp.int32)[None], c.astype(jnp.int32)[None]

    def start(parts, after):
        keep, send = pack(parts, s_here, after)
        got = mate(send, "section", 1)
        return [jnp.where(s == layer, keep, got) for layer in range(2)]

    flipped = [(jnp.swapaxes(w[0], 0, 1), True) for w in (key_weight, value_weight)]
    attn_start = start((w_query[0], *flipped, w_out[0]), [])
    first = attn_start[0]
    a = Gather(first)
    come = a.hop()
    ffn_start = start((w_gate[0], w_up[0], w_down[0]), [first])
    f = Gather(ffn_start[0])

    gains = behind(jnp.concatenate([gain_attn, gain_ffn], 0), first)
    pair = mate(gains, "section", 1)
    gains = jnp.concatenate([jnp.where(s == 0, gains, pair), jnp.where(s == 0, pair, gains)], 0)
    gains = jnp.stack([gains] + [ring(gains, -k) for k in range(1, n)], 1)
    gains = gains.reshape(4, n, 2, -1)
    gains = jnp.where(s == 0, gains, gains[:, :, ::-1]).transpose(0, 2, 1, 3).reshape(4, 1, -1)
    gains = gains.astype(F32)

    inputs, positions = behind(inputs, first), behind(positions, *come)
    order, back_order = feature_order(width, behind(s, *come))
    swaps = [swap_matrix(width_q, width_q), swap_matrix(width_q, width_kv)]
    x = lax.dynamic_index_in_dim(inputs, s, 0, keepdims=False)
    place = lax.dynamic_index_in_dim(positions, s, 0, keepdims=False)
    cot = lax.dynamic_index_in_dim(cotangent, s, 0, keepdims=False)
    piece = jnp.arange(count) ^ c
    token = (piece[:, None] * rows + jnp.arange(rows)[None, :]).reshape(-1)
    place = jnp.concatenate(
        [lax.dynamic_slice_in_dim(place, (c ^ k) * rows, rows) for k in range(count)]
    )
    tables = token_tables(place, width_q, width_kv)
    parity = lax.axis_index("row") % 2

    def order_of(side):
        half = tokens // 2
        return token + jnp.where(side == 0, jnp.where(token < half, 0, 2 * half), half)

    own_order = order_of(parity)
    orders = [own_order[None, :], jnp.concatenate([own_order, order_of(1 - parity)])[:, None]]

    point = meet(come)
    come = a.hop()
    x = enter(x, order, c_here, count, come + point + f.slots, True)
    a.hop()
    f.hop(*come)
    grad = enter(cot, order, c_here, count)

    kept, outs, gathers = [], [], []
    for layer in range(2):
        gain1, gain2 = gains[2 * layer], gains[2 * layer + 1]
        last = layer == 1
        gathers.append((a, f))
        come = meet(x[1:] + a.slots[-1:] + grad[:1]) if last else []
        n1, query, own = project(x, gain1, a.all(), tables, swaps, width_q, come)
        there = mate(own, "row", 1)
        come = f.hop(there)
        mixed, sums, y = attention(query, own, there, orders, a.all(), count)
        sent = received(y)
        f.hop(sent[-1])
        if not last:
            a, f_old = Gather(attn_start[1]), f
            a.hop(sent[-1])
        middle, n2 = add_and_norm(x[0], sent, gain2, come)
        n2 = gather_pieces(n2)
        point = meet(n2[1:] + f.slots[-1:] + a.slots[-1:])
        if not last:
            f = Gather(ffn_start[1])
            come = f.hop(n2[-1]) + a.hop(n2[-1])
        gate, up, hidden, y = feed_forward(
            n2, gathers[-1][1].all(), gathers[-1][1].all(), point
        )
        kept.append((x[0], n1, query, own, there, mixed, sums, middle, n2, gate, up, hidden))
        if not last:
            sent = received(y)
            a.hop(sent[-1])
            x = gather_pieces(add_up(middle, sent, come))
            outs.append(x)

    def exchange(values):
        return mate(choose(values, s_here), "section", 1)

    left, parts, gain_parts = [None, None], [None, None], [None, None]
    last_y, s_a, come = y, None, []
    for layer in (1, 0):
        a, f = gathers[layer]
        x, n1, query, own, there, mixed, sums, middle, n2, gate, up, hidden = kept[layer]
        gain1, gain2 = gains[2 * layer], gains[2 * layer + 1]
        if s_a:
            s_a.begin(grad[-1])
            s_d.begin(grad[-1])
        grad_gu, y = feed_forward_back(grad, gate, up, f.all(), f.all(), come)
        sent = received(y)
        come = s_a.finish(sent[-1]) + s_d.finish(sent[-1]) if s_a else []
        s_f = Scatter([(n2, grad_gu)], units // 2)
        come += s_f.made
        s_f.begin(sent[-1])
        g_gain2, grad_middle, grad_attn = norm_back(middle, sent, gain2, grad[0], come)
        s_d = Scatter([(grad, behind(hidden, grad_attn))], units // 2)
        grad_attn = gather_pieces(grad_attn)
        come = s_d.made + s_f.finish(grad_attn[-1])
        s_d.begin(grad_attn[-1])
        if s_a:
            s_a.begin(grad_attn[-1])
        grad_query, grad_own, grad_there = attention_back(
            grad_attn, query, own, there, sums, orders, a.all(), come
        )
        if layer == 1:
            last_y = received([behind(p, grad_attn[-1]) for p in last_y])
            left[0] = leave([behind(p, grad_there) for p in outs[0]], back_order, c_here)
            come = last_y[1:] + [left[0]]
        else:
            last_y = add_up(kept[1][7], last_y, [grad_attn[0]])
            outs.append(gather_pieces(behind(last_y, grad_attn[-1])))
            left[1] = leave([behind(p, grad_there) for p in grad], back_order, c_here)
            come = outs[1][1:] + [left[1]]
        back = mate(grad_there, "row", 1)
        come += s_d.finish(back) + (s_a.finish(back) if s_a else [])
        s_f.begin(back)
        s_d.begin(back)
        y, grad_qkv = project_back(
            grad_query, grad_own, back, a.all(), tables, swaps, count, come
        )
        sent = received(y)
        come = s_f.finish(sent[-1]) + s_d.finish(sent[-1])
        s_a = Scatter([([n1], grad_qkv), (grad_attn, mixed)], width_q)
        s_f.begin(sent[-1])
        s_a.begin(sent[-1])
        g_gain1, _, grad = norm_back(x, sent, gain1, grad_middle, come + s_a.made)
        mark = meet([grad])
        grad = gather_pieces(grad)
        come = s_f.finish(grad[-1]) + s_a.finish(grad[-1])
        parts[layer] = (s_a, s_f, s_d)
        gain_parts[layer] = (g_gain1, g_gain2)

    acts = [left[0], leave([behind(p, *mark) for p in outs[1]], back_order, c_here)]
    gain_grads = jnp.concatenate(list(gain_parts[0]) + list(gain_parts[1]), 0)
    gain_slots = gather_gains(gain_grads, s_here)
    point = meet(grad[1:] + acts[1:] + come + mark + gain_slots)
    s_a.begin(*point)
    s_d.begin(*point)
    mark = meet(point)
    grads = [leave([behind(p, *mark) for p in grad], back_order, c_here, path=True), left[1]]
    grads_got = exchange(grads)
    acts_got = exchange([behind(v, *mark) for v in acts])
    wide = [p[1].moving for p in parts]
    wide_got = exchange([behind(v, *mark) for v in wide])
    gain_grads = reduce_gains([behind(v, *mark) for v in gain_slots], s_here)
    point = meet(s_a.finish(grads[0]) + s_d.finish(grads[0]) + gain_grads + mark)
    s_a.begin(*point)
    mark = meet(point)
    acts = place_out([behind(v, *mark) for v in acts], acts_got, s_here)
    grads = place_out([behind(v, *mark) for v in grads], grads_got, s_here)
    g_gate, g_up = unpack([behind(v, *mark) for v in wide], wide_got, s_here, (units, units))
    s_a.finish(grads, acts, g_up)
    gain_grads = gain_grads[0] + mate(gain_grads[1], "section", 1)
    heads, narrow = ([p[k].moving for p in parts] for k in (0, 2))
    heads_got, narrow_got = exchange(heads), exchange(narrow)
    point = meet([heads_got, narrow_got, g_up, acts, grads])
    (g_down,) = unpack(narrow, narrow_got, s_here, (units,), point)
    g_query, g_key, g_value, g_out = unpack(
        heads, heads_got, s_here, (width_q, width_kv, width_kv, width_q), point, (1, 2)
    )
    g_key, g_value = jnp.swapaxes(g_key, 0, 1), jnp.swapaxes(g_value, 0, 1)
    return (
        acts[None],
        grads[None],
        *[g[None] for g in (g_query, g_key, g_value, g_out, g_gate, g_up, g_down)],
        gain_grads[0:1],
        gain_grads[1:2],
    )


def solution(mesh):
    placed = (
        P(None, "row", None),
        P(None, "row"),
        *[P("section", "row", "col")] * 7,
        *[P("section", "row")] * 2,
        P(None, "row", None),
    )
    return jax.shard_map(
        body,
        mesh=mesh,
        in_specs=placed,
        out_specs=(
            *[P("section", None, "row", None)] * 2,
            *[P("section", "row", "col")] * 7,
            *[P("section", "row")] * 2,
        ),
        check_vma=False,
    )
```
